256 devices in a mesh: seq: 64 (over x, z, core), head: 4 (over y).
Axes of the slice: x: 4, y: 4, z: 8, core: 2. Of those that a mesh axis runs over, the one named last changes fastest.
Arguments:
- query_input: bfloat16 [16384, 2048], P('seq', 'head'), may hold values from -6 to 6
- key_input: bfloat16 [16384, 2048], P('seq', 'head'), may hold values from -6 to 6
- value_input: bfloat16 [16384, 2048], P('seq', 'head'), may hold values from -6 to 6
- out_weight: bfloat16 [4096, 2048], P('seq', 'head'), may hold values from -0.125 to 0.125
- cotangent: bfloat16 [16384, 4096], P('seq', 'head'), may hold values from -16 to 16
Outputs:
- layer_out: bfloat16 [16384, 4096], P('seq', 'head')
- query_grad: bfloat16 [16384, 2048], P('seq', 'head')
- key_grad: bfloat16 [16384, 2048], P('seq', 'head')
- value_grad: bfloat16 [16384, 2048], P('seq', 'head')
- weight_grad: float32 [4096, 2048], P('seq', 'head')
The draws below stay inside these ranges and needn't reach their ends.
All inputs are finite; a program needn't handle non-finite values.
Results may differ from the reference program's by a relative error of at most 0.018.
Values may be sent and summed in bfloat16 or wider, within the bound.
A program may use at most 128 MiB of HBM per device.

```python
import jax
import jax.numpy as jnp
from jax import lax

D = 4096
HEADS = 16
HEAD_DIM = 128
SEQ_LEN = 16384
BLOCK = 256
N_HEAD = 4


def raised(values, stream_key, source, target, blocks, factor):
    def block_of(position):
        return (jnp.arange(values.shape[position]) // (values.shape[position] // blocks)).reshape((-1,) + (1,) * (values.ndim - 1 - position))

    first = jax.random.permutation(stream_key, blocks)[block_of(target)]
    second = (block_of(target) + blocks // 2) % blocks
    return jnp.where((block_of(source) == first) | (block_of(source) == second), factor * values, values)


def block_levels(rng, shape, cuts, smallest, largest):
    def one(position, parts):
        draws = jax.random.uniform(jax.random.fold_in(jax.random.fold_in(rng, 6), position), (parts,), jnp.float32, smallest / len(cuts), largest / len(cuts))
        return jnp.repeat(jnp.exp(draws), shape[position] // parts).reshape((-1,) + (1,) * (len(shape) - position - 1))

    loudness = one(*cuts[0])
    for cut in cuts[1:]:
        loudness = loudness * one(*cut)
    return loudness


def scatter_about(stream_key, extent, scale, most, cuts=(), kind=jnp.bfloat16):
    array = scale * jax.random.normal(stream_key, extent, jnp.float32)
    if cuts:
        array = array * block_levels(stream_key, extent, cuts, -0.22, 0.18)
    return jnp.clip(array, -most, most).astype(kind)


def gaussian_with(stream_key, dims, spread, reach, cuts, heavy, kind=jnp.bfloat16):
    entries = spread * jax.random.normal(stream_key, dims, jnp.float32)
    if cuts:
        entries = entries * block_levels(stream_key, dims, cuts, -0.22, 0.18)
    return jnp.clip(raised(entries, jax.random.fold_in(stream_key, 3), *heavy), -reach, reach).astype(kind)


def setup_inputs(seed: int = 0) -> dict:
    streams_of = jax.random.split(jax.random.key(seed), 6)
    return {
        "query_input": scatter_about(streams_of[0], (SEQ_LEN, HEADS * HEAD_DIM), 1.0, 6.0, ((0, 64), (1, 4))),
        "key_input": scatter_about(streams_of[1], (SEQ_LEN, HEADS * HEAD_DIM), 1.0, 6.0, ((0, 64), (1, 4))),
        "value_input": scatter_about(streams_of[2], (SEQ_LEN, HEADS * HEAD_DIM), 1.0, 6.0, ((0, 64), (1, 4))),
        "out_weight": scatter_about(streams_of[3], (D, HEADS * HEAD_DIM), (HEADS * HEAD_DIM) ** -0.5, 0.125, ((0, 64), (1, 4))),
        "cotangent": gaussian_with(streams_of[4], (SEQ_LEN, D), 1.0, 16.0, ((0, 64), (1, 4)), (0, 1, 64, 4.0)),
    }


highest = lax.Precision.HIGHEST
epsilon = 1e-06

def features(raw_input):
    values = raw_input.astype(jnp.float32)
    return jnp.where(values > 0, values + 1.0, jnp.exp(jnp.minimum(values, 0.0)))

def feature_slope(raw_input):
    values = raw_input.astype(jnp.float32)
    return jnp.where(values > 0, 1.0, jnp.exp(jnp.minimum(values, 0.0)))

def reference(query_input, key_input, value_input, out_weight, cotangent):
    full_width = HEADS * HEAD_DIM
    block_total = SEQ_LEN // BLOCK

    def blocks_of(tensor_in):
        return tensor_in.reshape(block_total, BLOCK, HEADS, HEAD_DIM)
    q_feat = blocks_of(features(query_input).astype(jnp.bfloat16))
    k_feat = blocks_of(features(key_input).astype(jnp.bfloat16))
    v_vals = blocks_of(value_input)
    causal = jnp.tril(jnp.ones((BLOCK, BLOCK), jnp.float32))
    zero_state = jnp.zeros((HEADS, HEAD_DIM, HEAD_DIM), jnp.float32)

    def forward_step(carry_state, pieces):
        q_blk, k_blk, v_blk = pieces
        q_wide = q_blk.astype(jnp.float32)
        k_wide = k_blk.astype(jnp.float32)
        v_wide = v_blk.astype(jnp.float32)
        scores = (jnp.einsum('the,she->hts', q_wide, k_wide, precision=highest) * causal).astype(jnp.bfloat16)
        attended = jnp.einsum('hts,shf->thf', scores.astype(jnp.float32), v_wide, precision=highest)
        attended = attended + jnp.einsum('the,hef->thf', q_wide, carry_state, precision=highest)
        new_state = carry_state + jnp.einsum('the,thf->hef', k_wide, v_wide, precision=highest)
        return (new_state, (attended, carry_state, scores))
    final_state, (attended, prior_state, block_scores) = lax.scan(forward_step, zero_state, (q_feat, k_feat, v_vals))
    inv_rms = lax.rsqrt(lax.optimization_barrier(jnp.mean(attended * attended, axis=-1, keepdims=True)) + epsilon)
    unit_rms = attended * inv_rms
    normed = unit_rms.reshape(SEQ_LEN, full_width).astype(jnp.bfloat16)
    group_width = full_width // N_HEAD
    summed = jnp.zeros((SEQ_LEN, D), jnp.float32)
    for group_index in range(N_HEAD):
        low_col = group_index * group_width
        group_part = lax.dot_general(normed[:, low_col:low_col + group_width], out_weight[:, low_col:low_col + group_width], (((1,), (1,)), ((), ())), preferred_element_type=jnp.float32)
        rounded = lax.optimization_barrier(group_part.astype(jnp.bfloat16))
        summed = summed + rounded.astype(jnp.float32)
    layer_out = summed.astype(jnp.bfloat16)
    weight_grad = lax.dot_general(cotangent, normed, (((0,), (0,)), ((), ())), preferred_element_type=jnp.float32) * SEQ_LEN ** (-0.5)
    upstream = blocks_of(jnp.dot(cotangent, out_weight, preferred_element_type=jnp.float32))
    inner_term = lax.optimization_barrier(jnp.mean(upstream * unit_rms, axis=-1, keepdims=True))
    d_att = (inv_rms * (upstream - unit_rms * inner_term)).astype(jnp.bfloat16)

    def backward_step(after_state, pieces):
        q_blk, k_blk, v_blk, d_blk, carry_state, score_blk = pieces
        q_wide = q_blk.astype(jnp.float32)
        k_wide = k_blk.astype(jnp.float32)
        v_wide = v_blk.astype(jnp.float32)
        d_wide = d_blk.astype(jnp.float32)
        s_wide = score_blk.astype(jnp.float32)
        d_scores = (jnp.einsum('thf,shf->hts', d_wide, v_wide, precision=highest) * causal).astype(jnp.bfloat16).astype(jnp.float32)
        q_grad = jnp.einsum('hts,she->the', d_scores, k_wide, precision=highest)
        q_grad = q_grad + jnp.einsum('hef,thf->the', carry_state, d_wide, precision=highest)
        k_grad = jnp.einsum('hts,the->she', d_scores, q_wide, precision=highest)
        k_grad = k_grad + jnp.einsum('hef,shf->she', after_state, v_wide, precision=highest)
        v_grad = jnp.einsum('hts,thf->shf', s_wide, d_wide, precision=highest)
        v_grad = v_grad + jnp.einsum('hef,she->shf', after_state, k_wide, precision=highest)
        new_after = after_state + jnp.einsum('the,thf->hef', q_wide, d_wide, precision=highest)
        return (new_after, (q_grad, k_grad, v_grad))
    first_after, (q_grad, k_grad, v_grad) = lax.scan(backward_step, zero_state, (q_feat, k_feat, v_vals, d_att, prior_state, block_scores), reverse=True)
    query_grad = (q_grad * blocks_of(feature_slope(query_input))).reshape(SEQ_LEN, full_width).astype(jnp.bfloat16)
    key_grad = (k_grad * blocks_of(feature_slope(key_input))).reshape(SEQ_LEN, full_width).astype(jnp.bfloat16)
    value_grad = v_grad.reshape(SEQ_LEN, full_width).astype(jnp.bfloat16)
    return (layer_out, query_grad, key_grad, value_grad, weight_grad)
```

```python
import functools

import jax
import jax.numpy as jnp
from jax import lax
from jax.experimental import pallas as pl
from jax.experimental.pallas import tpu as pltpu
from jax.sharding import Mesh
from jax.sharding import PartitionSpec as P

SEQ = ("seq_0", "seq_1", "seq_2")
NX, NZ, NC, NY = 4, 8, 2, 4
HD = 128
HEADS = 4
ROWS = 256
WIDTH = HEADS * HD
FEATS = 1024
EPS = 1e-06
WROWS = 64
WA = 16
COPIES = 176
MESH = pl.DeviceIdType.MESH
f32 = jnp.float32
bf16 = jnp.bfloat16


def nn(a, b):
    return lax.dot_general(a, b, (((1,), (0,)), ((), ())), preferred_element_type=f32)


def nt(a, b):
    return lax.dot_general(a, b, (((1,), (1,)), ((), ())), preferred_element_type=f32)


def tn(a, b):
    return lax.dot_general(a, b, (((0,), (0,)), ((), ())), preferred_element_type=f32)


def kernel(
    grad_scale,
    q_ref, k_ref, v_ref, w_ref, c_ref,
    lo_ref, qg_ref, kg_ref, vg_ref, dw_ref,
    qf, kf, scores, att, unit, inv, normed, datt, prior, kacc, vacc,
    state, own_b, sib_b, chip, zsend, zrecv, tsend, trecv, psend, pre,
    wall, call, csib, lsend, lrecv, ntown, ntsend, ntsib,
    xsend, xrecv, xsum, dsend, drecv, rsend, rrecv, zown, esend, erecv, mine, tsib_recv,
    ssem, rsem, lsem,
):
    x, z, c, y = (lax.axis_index(a) for a in (*SEQ, "head"))
    s = 1 - 2 * c

    def at(dx=0, dz=0, dc=0, dy=0):
        return (
            lax.rem(x + dx + NX, NX),
            lax.rem(z + dz + NZ, NZ),
            lax.rem(c + dc, NC),
            lax.rem(y + dy + NY, NY),
        )

    def zat(offset):
        return lax.rem(z + offset + 2 * NZ, NZ)

    peers = [at(dc=1)]
    peers += [at(dz=j) for j in range(1, NZ)]
    peers += [at(dx=j) for j in range(1, NX)]
    peers += [at(dy=j) for j in range(1, NY)]

    made = []

    def send(src, dst, device):
        n = len(made)
        copy = pltpu.make_async_remote_copy(
            src_ref=src, dst_ref=dst, send_sem=ssem.at[n], recv_sem=rsem.at[n],
            device_id=device, device_id_type=MESH,
        )
        copy.start()
        made.append(copy)
        return copy

    def cols(h):
        return pl.ds(h * HD, HD)

    def rows(h):
        return pl.ds(h * HD, HD)

    def phi(ref, h):
        a = ref[:, cols(h)].astype(f32)
        return jnp.where(a > 0, a + 1.0, jnp.exp(jnp.minimum(a, 0.0)))

    def slope(ref, h):
        a = ref[:, cols(h)].astype(f32)
        return jnp.where(a > 0, 1.0, jnp.exp(jnp.minimum(a, 0.0)))

    def causal():
        t = lax.broadcasted_iota(jnp.int32, (ROWS, ROWS), 0)
        u = lax.broadcasted_iota(jnp.int32, (ROWS, ROWS), 1)
        return u <= t

    half = 2 * HD
    piece = half // NZ
    lo_row = pl.multiple_of(half * c, half)

    def scan_begin(i):
        own_b[i] = state[...].astype(bf16)
        return send(own_b.at[i], sib_b.at[i], at(dc=1))

    def scan_chip(i, copy):
        copy.wait_recv()
        total = own_b[i, pl.ds(lo_row, half)].astype(f32) + sib_b[i, pl.ds(lo_row, half)].astype(f32)
        chip[...] = total
        zsend[i] = total.astype(bf16)
        out = []
        for j in range(1, NZ):
            d = zat(j)
            out.append(send(zsend.at[i, pl.ds(pl.multiple_of(d * piece, piece), piece)], zrecv.at[i, z], at(dz=j)))
        return out

    def scan_total(i, copies, reverse):
        for copy in copies:
            copy.wait_recv()
        zrecv[i, z] = zsend[i, pl.ds(pl.multiple_of(z * piece, piece), piece)]
        running = jnp.zeros((piece, HD), f32)
        inner = [None] * NZ
        for o in reversed(range(NZ)) if reverse else range(NZ):
            inner[o] = running
            running = running + zrecv[i, o].astype(f32)
        tsend[i] = running.astype(bf16)
        out = [send(tsend.at[i], trecv.at[i, x], at(dx=j)) for j in range(1, NX)]
        trecv[i, x] = tsend[i]
        return inner, out

    def scan_back(i, state_in, reverse):
        inner, copies = state_in
        for copy in copies:
            copy.wait_recv()
        outer = jnp.zeros((piece, HD), f32)
        for o in range(NX):
            passed = (o > x) if reverse else (o < x)
            outer = outer + jnp.where(passed, trecv[i, o].astype(f32), 0.0)
        for o in range(NZ):
            psend[i, o] = (inner[o] + outer).astype(bf16)
        place = pl.ds(pl.multiple_of(half * c + piece * z, piece), piece)
        out = [send(psend.at[i, zat(j)], pre.at[i, place], at(dz=j)) for j in range(1, NZ)]
        pre[i, place] = psend[i, z]
        return out

    def scan_share(i, copies):
        for copy in copies:
            copy.wait_recv()
        return send(pre.at[i, pl.ds(lo_row, half)], pre.at[i, pl.ds(lo_row, half)], at(dc=1))

    def scan_end(i, copy, reverse):
        copy.wait_recv()
        takes = (c == 0) if reverse else (c == 1)
        state[...] = pre[i].astype(f32) + jnp.where(takes, sib_b[i].astype(f32), 0.0)

    barrier = pltpu.get_barrier_semaphore()
    for peer in peers:
        pl.semaphore_signal(barrier, inc=1, device_id=peer, device_id_type=MESH)
    own_cot = pltpu.make_async_copy(c_ref, call.at[y], lsem.at[0])
    own_cot.start()
    wall[x, z, c] = w_ref[...]
    for h in range(HEADS):
        kh = phi(k_ref, h).astype(bf16)
        kf[:, cols(h)] = kh
        state[rows(h), :] = tn(kh, v_ref[:, cols(h)])
    pl.semaphore_wait(barrier, len(peers))

    scan = scan_begin(0)
    part_a = pl.ds(0, WA)
    part_b = pl.ds(WA, WROWS - WA)
    xa = [send(wall.at[x, z, c, part_a], wall.at[x, z, c, part_a], at(dx=j)) for j in range(1, NX)]

    def b_across(origin):
        return [
            send(wall.at[x, origin, c, part_b], wall.at[x, origin, c, part_b], at(dx=j)) for j in range(1, NX)
        ]

    def b_step(origin, way):
        return send(wall.at[x, origin, c, part_b], wall.at[x, origin, c, part_b], at(dz=way))

    def a_step(origin, way):
        return send(wall.at[:, origin, c, part_a], wall.at[:, origin, c, part_a], at(dz=way))

    bm = [b_step(z, s)]
    bo = [b_step(z, -s)]
    scan = scan_chip(0, scan)
    cot_y = [send(c_ref, call.at[y], at(dy=j)) for j in (2, 1, 3)]
    xb = {0: b_across(z)}
    cot_c = [send(c_ref, csib.at[y], at(dc=1))]

    am, ao = [], []

    def serve_b(i):
        bm[i].wait_recv()
        if i < 3:
            bm.append(b_step(zat(-s * (i + 1)), s))
        if i < 3:
            bo[i].wait_recv()
            if i < 2:
                bo.append(b_step(zat(s * (i + 1)), -s))
            xb[-i - 1] = b_across(zat(s * (i + 1)))
        xb[i + 1] = b_across(zat(-s * (i + 1)))

    def serve_a0():
        for copy in xa:
            copy.wait_recv()
        am.append(a_step(z, s))
        ao.append(a_step(z, -s))

    def serve_a(i):
        am[i].wait_recv()
        if i < 3:
            am.append(a_step(zat(-s * (i + 1)), s))
        if i < 3:
            ao[i].wait_recv()
            if i < 2:
                ao.append(a_step(zat(s * (i + 1)), -s))

    wsib = []

    def share_w(k):
        for copy in xb[k]:
            copy.wait_recv()
        origin = zat(-s * k)
        wsib.append(send(wall.at[:, origin, c], wall.at[:, origin, c], at(dc=1)))

    def intra(h):
        qh = phi(q_ref, h).astype(bf16)
        qf[:, cols(h)] = qh
        sc = jnp.where(causal(), nt(qh, kf[:, cols(h)]), 0.0).astype(bf16)
        scores[h] = sc
        att[:, cols(h)] = nn(sc, v_ref[:, cols(h)])

    intra(0)
    intra(1)
    serve_b(0)
    serve_a0()
    intra(2)
    intra(3)
    scan = scan_total(0, scan, False)
    serve_b(1)
    serve_a(0)
    scan = scan_back(0, scan, False)
    serve_b(2)
    serve_a(1)
    serve_b(3)
    share_w(0)
    scan = scan_share(0, scan)
    serve_a(2)
    scan_end(0, scan, False)

    for h in range(HEADS):
        st = state[rows(h), :].astype(bf16)
        a = att[:, cols(h)] + nn(qf[:, cols(h)], st)
        r = lax.rsqrt(jnp.mean(a * a, axis=-1, keepdims=True) + EPS)
        u = a * r
        unit[:, cols(h)] = u
        inv[:, cols(h)] = jnp.broadcast_to(r, (ROWS, HD))
        n = u.astype(bf16)
        normed[:, cols(h)] = n
        prior[rows(h), :] = st
        t = u.T.astype(bf16)
        ntsend[h // 2, pl.ds((h % 2) * HD, HD), :] = t
    nt_copy = send(ntsend.at[1 - c], ntsib, at(dc=1))
    ntown[...] = ntsend[c]

    for k in (1, -1, 2, -2):
        share_w(k)
    serve_a(3)
    for k in (3, -3, 4):
        share_w(k)
    for copy in wsib:
        copy.wait_recv()
    own_cot.wait()

    def weight(b):
        return wall[b].reshape(FEATS, WIDTH)

    lcopy = []
    for j in (2, 1, 3):
        d = lax.rem(y + j, NY)
        lsend[j] = nt(normed[...], weight(d)).astype(bf16)
        lcopy.append(send(lsend.at[j], lrecv.at[j - 1], at(dy=j)))
    lsend[0] = nt(normed[...], weight(y)).astype(bf16)

    for copy, j in zip(cot_y, (2, 1, 3)):
        copy.wait_recv()
        b = lax.rem(y - j + NY, NY)
        cot_c.append(send(call.at[b], csib.at[b], at(dc=1)))
    up = nn(call[0], weight(0))
    for b in range(1, NY):
        up = up + nn(call[b], weight(b))
    for h in range(HEADS):
        u = unit[:, cols(h)]
        d = up[:, h * HD : (h + 1) * HD]
        m = jnp.mean(d * u, axis=-1, keepdims=True)
        da = (inv[:, cols(h)] * (d - u * m)).astype(bf16)
        datt[:, cols(h)] = da
        state[rows(h), :] = tn(qf[:, cols(h)], da)
    scan = scan_begin(1)

    for copy in cot_c:
        copy.wait_recv()
    nt_copy.wait_recv()
    scan = scan_chip(1, scan)

    def x_part(b):
        return nn(ntown[pl.ds(HD, HD), :], call[b]) + nn(ntsib[pl.ds(HD, HD), :], csib[b])

    def z_part(d, b):
        at_d = pl.ds(pl.multiple_of(d * HD, HD), HD)
        return nn(ntown[pl.ds(0, HD), :], call[b, :, at_d]) + nn(ntsib[pl.ds(0, HD), :], csib[b, :, at_d])

    rm, ro = [], []

    def ring(i):
        far = zat(s * (4 - i))
        for b in range(NX):
            p = z_part(far, b)
            if i:
                p = p + rrecv[i - 1, b].astype(f32)
            rsend[i, b] = p.astype(bf16)
        rm.append(send(rsend.at[i], rrecv.at[i], at(dz=s)))
        if i < 3:
            far = zat(-s * (3 - i))
            for b in range(NX):
                p = z_part(far, b)
                if i:
                    p = p + rrecv[4 + i - 1, b].astype(f32)
                rsend[4 + i, b] = p.astype(bf16)
            ro.append(send(rsend.at[4 + i], rrecv.at[4 + i], at(dz=-s)))

    xcopy = []
    ring(0)
    for j in (2, 1, 3):
        d = lax.rem(x + j, NX)
        p = x_part(d).astype(bf16)
        for o in range(NZ):
            xsend[j - 1, o] = p[:, o * HD : (o + 1) * HD]
        xcopy.append(send(xsend.at[j - 1], xrecv.at[j - 1], at(dx=j)))
    p = x_part(x)
    for o in range(NZ):
        xsum[o] = p[:, o * HD : (o + 1) * HD]

    def grads(h):
        da = datt[:, cols(h)]
        vh = v_ref[:, cols(h)]
        ds = jnp.where(causal(), nt(da, vh), 0.0).astype(bf16)
        qg = nn(ds, kf[:, cols(h)]) + nt(da, prior[rows(h), :])
        qg_ref[:, cols(h)] = (qg * slope(q_ref, h)).astype(bf16)
        kacc[:, cols(h)] = tn(ds, qf[:, cols(h)])
        vacc[:, cols(h)] = tn(scores[h], da)

    rm[0].wait_recv()
    ro[0].wait_recv()
    ring(1)
    grads(0)
    scan = scan_total(1, scan, True)
    grads(1)
    rm[1].wait_recv()
    ro[1].wait_recv()
    ring(2)
    scan = scan_back(1, scan, True)
    grads(2)
    grads(3)
    rm[2].wait_recv()
    ro[2].wait_recv()
    ring(3)
    scan = scan_share(1, scan)
    for copy in xcopy:
        copy.wait_recv()
    dcopy = []
    for o in range(NZ):
        t = xsum[o]
        for j in range(NX - 1):
            t = t + xrecv[j, o].astype(f32)
        xsum[o] = t
        dsend[o] = t.astype(bf16)
    for j in range(1, NZ):
        dcopy.append(send(dsend.at[zat(j)], drecv.at[j - 1], at(dz=j)))
    scan_end(1, scan, True)
    for h in range(HEADS):
        st = state[rows(h), :].astype(bf16)
        kg = kacc[:, cols(h)] + nt(v_ref[:, cols(h)], st)
        kg_ref[:, cols(h)] = (kg * slope(k_ref, h)).astype(bf16)
        vg_ref[:, cols(h)] = (vacc[:, cols(h)] + nn(kf[:, cols(h)], st)).astype(bf16)

    rm[3].wait_recv()
    for b in range(NX):
        t = z_part(z, b) + rrecv[3, b].astype(f32) + rrecv[6, b].astype(f32)
        zown[b] = t
        esend[b] = t.astype(bf16)
    ecopy = [send(esend.at[lax.rem(x + j, NX)], erecv.at[j - 1], at(dx=j)) for j in range(1, NX)]

    total = lsend[0].astype(f32)
    for copy in lcopy:
        copy.wait_recv()
    for j in range(NY - 1):
        total = total + lrecv[j].astype(f32)
    lo_ref[...] = total.astype(bf16)

    for copy in ecopy:
        copy.wait_recv()
    t = zown[x]
    for j in range(NX - 1):
        t = t + erecv[j].astype(f32)
    mine[:, pl.ds(0, HD)] = t.T
    for copy in dcopy:
        copy.wait_recv()
    t = xsum[z]
    for j in range(NZ - 1):
        t = t + drecv[j].astype(f32)
    mine[:, pl.ds(HD, HD)] = t.T
    other = pl.multiple_of((1 - c) * WROWS, WROWS)
    last = send(mine.at[pl.ds(other, WROWS)], tsib_recv, at(dc=1))
    last.wait_recv()
    here = mine[pl.ds(pl.multiple_of(c * WROWS, WROWS), WROWS), :] * grad_scale
    there = tsib_recv[...] * grad_scale
    dw_ref[:, pl.ds(0, 2 * HD)] = jnp.where(c == 0, here, there)
    dw_ref[:, pl.ds(2 * HD, 2 * HD)] = jnp.where(c == 0, there, here)
    for copy in made:
        copy.wait_send()


def solution(mesh):
    split = Mesh(mesh.devices.reshape(NX, NZ, NC, NY), (*SEQ, "head"))
    placed = P(SEQ, "head")

    def shards(q, k, v, w, cot):
        shape = jax.ShapeDtypeStruct
        vm = pltpu.VMEM
        return pl.pallas_call(
            functools.partial(kernel, 16384.0**-0.5),
            out_shape=(
                shape((ROWS, FEATS), bf16),
                shape((ROWS, WIDTH), bf16),
                shape((ROWS, WIDTH), bf16),
                shape((ROWS, WIDTH), bf16),
                shape((WROWS, WIDTH), f32),
            ),
            in_specs=[pl.BlockSpec(memory_space=pltpu.VMEM)] * 5,
            out_specs=[pl.BlockSpec(memory_space=pltpu.VMEM)] * 5,
            scratch_shapes=[
                vm((ROWS, WIDTH), bf16),
                vm((ROWS, WIDTH), bf16),
                vm((HEADS, ROWS, ROWS), bf16),
                vm((ROWS, WIDTH), f32),
                vm((ROWS, WIDTH), f32),
                vm((ROWS, WIDTH), f32),
                vm((ROWS, WIDTH), bf16),
                vm((ROWS, WIDTH), bf16),
                vm((WIDTH, HD), bf16),
                vm((ROWS, WIDTH), f32),
                vm((ROWS, WIDTH), f32),
                vm((WIDTH, HD), f32),
                vm((2, WIDTH, HD), bf16),
                vm((2, WIDTH, HD), bf16),
                vm((2 * HD, HD), f32),
                vm((2, 2 * HD, HD), bf16),
                vm((2, NZ, 2 * HD // NZ, HD), bf16),
                vm((2, 2 * HD // NZ, HD), bf16),
                vm((2, NX, 2 * HD // NZ, HD), bf16),
                vm((2, NZ, 2 * HD // NZ, HD), bf16),
                vm((2, WIDTH, HD), bf16),
                vm((NX, NZ, NC, WROWS, WIDTH), bf16),
                vm((NY, ROWS, FEATS), bf16),
                vm((NY, ROWS, FEATS), bf16),
                vm((NY, ROWS, FEATS), bf16),
                vm((NY - 1, ROWS, FEATS), bf16),
                vm((2 * HD, ROWS), bf16),
                vm((2, 2 * HD, ROWS), bf16),
                vm((2 * HD, ROWS), bf16),
                vm((NX - 1, NZ, HD, HD), bf16),
                vm((NX - 1, NZ, HD, HD), bf16),
                vm((NZ, HD, HD), f32),
                vm((NZ, HD, HD), bf16),
                vm((NZ - 1, HD, HD), bf16),
                vm((7, NX, HD, HD), bf16),
                vm((7, NX, HD, HD), bf16),
                vm((NX, HD, HD), f32),
                vm((NX, HD, HD), bf16),
                vm((NX - 1, HD, HD), bf16),
                vm((HD, 2 * HD), f32),
                vm((WROWS, 2 * HD), f32),
                pltpu.SemaphoreType.DMA((COPIES,)),
                pltpu.SemaphoreType.DMA((COPIES,)),
                pltpu.SemaphoreType.DMA((1,)),
            ],
            compiler_params=pltpu.CompilerParams(
                collective_id=0, has_side_effects=True, vmem_limit_bytes=48 * 2**20
            ),
            name="layer_step",
        )(q, k, v, w, cot)

    return jax.shard_map(
        shards, mesh=split, in_specs=(placed,) * 5, out_specs=(placed,) * 5, check_vma=False
    )
```

```python
import functools

import jax
import jax.numpy as jnp
from jax import lax
from jax.experimental import pallas as pl
from jax.experimental.pallas import tpu as pltpu
from jax.sharding import Mesh
from jax.sharding import PartitionSpec as P

SEQ = ("seq_0", "seq_1", "seq_2")
NX, NZ, NC, NY = 4, 8, 2, 4
HD = 128
HEADS = 4
ROWS = 256
WIDTH = HEADS * HD
FEATS = 1024
EPS = 1e-06
WROWS = 64
WA = 16
ARRIVALS = 84
DEPARTURES = 20
MESH = pl.DeviceIdType.MESH
f32 = jnp.float32
bf16 = jnp.bfloat16


def nn(a, b):
    return lax.dot_general(a, b, (((1,), (0,)), ((), ())), preferred_element_type=f32)


def nt(a, b):
    return lax.dot_general(a, b, (((1,), (1,)), ((), ())), preferred_element_type=f32)


def tn(a, b):
    return lax.dot_general(a, b, (((0,), (0,)), ((), ())), preferred_element_type=f32)


def kernel(
    grad_scale,
    q_hbm, k_hbm, v_hbm, w_hbm, c_hbm,
    lo_ref, qg_ref, kg_ref, vg_ref, dw_ref,
    q_ref, k_ref, v_ref, qf, kf, scores, att, unit, inv, normed, datt, prior, kacc, vacc,
    state, own_b, sib_b, zsend, zrecv, tsend, trecv, psend, pre,
    wall, call, csib, lout, lsend, lrecv, lfar, ntown, ntsend, ntsib,
    pz, xsend, xrecv, xsum, dsend, drecv, rsend, rrecv, zown, esend, erecv, mine, tsib_recv,
    ssem, rsem, lsem,
):
    x, z, c, y = (lax.axis_index(a) for a in (*SEQ, "head"))
    s = 1 - 2 * c

    def at(dx=0, dz=0, dc=0, dy=0):
        return (
            lax.rem(x + dx + NX, NX),
            lax.rem(z + dz + NZ, NZ),
            lax.rem(c + dc, NC),
            lax.rem(y + dy + NY, NY),
        )

    def zat(offset):
        return lax.rem(z + offset + 2 * NZ, NZ)

    peers = [at(dc=1)]
    peers += [at(dz=j) for j in range(1, NZ)]
    peers += [at(dx=j) for j in range(1, NX)]
    peers += [at(dy=j) for j in range(1, NY)]

    kinds = {}
    arrivals = []

    def arrival():
        arrivals.append(None)
        return rsem.at[len(arrivals) - 1]

    def send(src, dst, device, kind, landed=None):
        copy = pltpu.make_async_remote_copy(
            src_ref=src, dst_ref=dst, send_sem=ssem.at[kinds.setdefault(kind, len(kinds))],
            recv_sem=arrival() if landed is None else landed,
            device_id=device, device_id_type=MESH,
        )
        copy.start()
        return copy

    def await_all(ref, sem):
        pltpu.make_async_copy(ref, ref, sem).wait()

    def sent(kind, ref):
        await_all(ref, ssem.at[kinds.pop(kind)])

    def cols(h):
        return pl.ds(h * HD, HD)

    def rows(h):
        return pl.ds(h * HD, HD)

    def phi(ref, h):
        a = ref[:, cols(h)].astype(f32)
        return jnp.where(a > 0, a + 1.0, jnp.exp(jnp.minimum(a, 0.0)))

    def slope(ref, h):
        a = ref[:, cols(h)].astype(f32)
        return jnp.where(a > 0, 1.0, jnp.exp(jnp.minimum(a, 0.0)))

    def causal():
        t = lax.broadcasted_iota(jnp.int32, (ROWS, ROWS), 0)
        u = lax.broadcasted_iota(jnp.int32, (ROWS, ROWS), 1)
        return u <= t

    half = 2 * HD
    piece = half // NZ
    lo_row = pl.multiple_of(half * c, half)

    def scan_begin(i):
        own_b[i] = state[...].astype(bf16)
        return send(own_b.at[i], sib_b.at[i], at(dc=1), "own")

    def scan_chip(i, copy):
        copy.wait_recv()
        total = own_b[i, pl.ds(lo_row, half)].astype(f32) + sib_b[i, pl.ds(lo_row, half)].astype(f32)
        zsend[i] = total.astype(bf16)
        landed = arrival()
        for j in range(1, NZ):
            rows_of = pl.ds(pl.multiple_of(zat(j) * piece, piece), piece)
            send(zsend.at[i, rows_of], zrecv.at[i, z], at(dz=j), "chip", landed)
        return landed

    def scan_total(i, landed, reverse):
        await_all(zrecv.at[i, pl.ds(0, NZ - 1)], landed)
        zrecv[i, z] = zsend[i, pl.ds(pl.multiple_of(z * piece, piece), piece)]
        running = jnp.zeros((piece, HD), f32)
        inner = [None] * NZ
        for o in reversed(range(NZ)) if reverse else range(NZ):
            inner[o] = running
            running = running + zrecv[i, o].astype(f32)
        tsend[i] = running.astype(bf16)
        landed = arrival()
        for j in range(1, NX):
            send(tsend.at[i], trecv.at[i, x], at(dx=j), "total", landed)
        return inner, landed

    def scan_back(i, state_in, reverse):
        inner, landed = state_in
        await_all(trecv.at[i, pl.ds(0, NX - 1)], landed)
        trecv[i, x] = tsend[i]
        outer = jnp.zeros((piece, HD), f32)
        for o in range(NX):
            passed = (o > x) if reverse else (o < x)
            outer = outer + jnp.where(passed, trecv[i, o].astype(f32), 0.0)
        for o in range(NZ):
            psend[i, o] = (inner[o] + outer).astype(bf16)
        place = pl.ds(pl.multiple_of(half * c + piece * z, piece), piece)
        landed = arrival()
        for j in range(1, NZ):
            send(psend.at[i, zat(j)], pre.at[i, place], at(dz=j), "back", landed)
        pre[i, place] = psend[i, z]
        return landed

    def scan_share(i, landed):
        await_all(psend.at[i, pl.ds(0, NZ - 1)], landed)
        return send(pre.at[i, pl.ds(lo_row, half)], pre.at[i, pl.ds(lo_row, half)], at(dc=1), "share")

    def scan_end(i, copy, reverse):
        copy.wait_recv()
        takes = (c == 0) if reverse else (c == 1)
        state[...] = pre[i].astype(f32) + jnp.where(takes, sib_b[i].astype(f32), 0.0)

    barrier = pltpu.get_barrier_semaphore()
    for peer in peers:
        pl.semaphore_signal(barrier, inc=1, device_id=peer, device_id_type=MESH)
    def load(i, src, dst):
        copy = pltpu.make_async_copy(src, dst, lsem.at[i])
        copy.start()
        return copy

    k_in = load(0, k_hbm, k_ref)
    v_in = load(1, v_hbm, v_ref)
    w_in = load(2, w_hbm, wall.at[x, z, c])
    c_in = load(3, c_hbm, call.at[y])
    q_in = load(4, q_hbm, q_ref)
    k_in.wait()
    v_in.wait()
    for h in range(HEADS):
        kh = phi(k_ref, h).astype(bf16)
        kf[:, cols(h)] = kh
        state[rows(h), :] = tn(kh, v_ref[:, cols(h)])
    for copy in (w_in, c_in, q_in):
        copy.wait()
    pl.semaphore_wait(barrier, len(peers))

    scan = scan_begin(0)
    part_a = pl.ds(0, WA)
    part_b = pl.ds(WA, WROWS - WA)
    xa = arrival()
    for j in range(1, NX):
        send(wall.at[x, z, c, part_a], wall.at[x, z, c, part_a], at(dx=j), "xa", xa)
    left, right = pl.ds(0, 2 * HD), pl.ds(2 * HD, 2 * HD)
    left_x, right_x = lax.rem(x + NX - 1, NX), lax.rem(x + 1, NX)

    def place(k):
        return zat(-s * k)

    def b_across(k):
        block = wall.at[x, place(k), c, part_b]
        return send(block, block, at(dx=1), "bx"), send(block, block, at(dx=-1), "bx")

    def b_relay(k):
        up_copy, down_copy = xb[k]
        landed = arrival()
        up_copy.wait_recv()
        block = wall.at[left_x, place(k), c, part_b, left]
        send(block, block, at(dx=1), "br", landed)
        down_copy.wait_recv()
        block = wall.at[right_x, place(k), c, part_b, right]
        send(block, block, at(dx=-1), "br", landed)
        xr[k] = landed

    def b_step(origin, way):
        block = wall.at[x, origin, c, part_b]
        return send(block, block, at(dz=way), "b")

    def a_step(origin, way):
        group = wall.at[:, origin, c, part_a]
        return send(group, group, at(dz=way), "a")

    bm = [b_step(z, s)]
    bo = [b_step(z, -s)]
    top, bottom = pl.ds(0, ROWS // 2), pl.ds(ROWS // 2, ROWS // 2)
    up_y, down_y = lax.rem(y + 1, NY), lax.rem(y + NY - 1, NY)
    far_y = lax.rem(y + 2, NY)

    def cot(b, part, way):
        return send(call.at[b, part], call.at[b, part], at(dy=way), "cot")

    p_top = cot(y, top, 1)
    m_bottom = cot(y, bottom, -1)
    p_bottom = cot(y, bottom, 1)
    m_top = cot(y, top, -1)
    xb, xr = {0: b_across(0)}, {}
    scan = scan_chip(0, scan)

    def cot_share(b):
        return send(call.at[b], csib.at[b], at(dc=1), "cot2")

    cot_c = {0: cot_share(y)}
    am, ao = [], []

    def serve_b(i):
        bm[i].wait_recv()
        if i < 3:
            bm.append(b_step(place(i + 1), s))
            bo[i].wait_recv()
            if i < 2:
                bo.append(b_step(place(-i - 1), -s))
            xb[-i - 1] = b_across(-i - 1)
        xb[i + 1] = b_across(i + 1)

    def serve_a0():
        await_all(wall.at[pl.ds(0, NX - 1), 0, 0, part_a], xa)
        am.append(a_step(z, s))
        ao.append(a_step(z, -s))

    def serve_a(i):
        am[i].wait_recv()
        if i < 3:
            am.append(a_step(place(i + 1), s))
            ao[i].wait_recv()
            if i < 2:
                ao.append(a_step(place(-i - 1), -s))

    wsib = arrival()

    def share_w(k):
        await_all(wall.at[0, 0, 0, part_b], xr[k])
        group = wall.at[:, place(k), c]
        send(group, group, at(dc=1), "wshare", wsib)

    def intra(h):
        qh = phi(q_ref, h).astype(bf16)
        qf[:, cols(h)] = qh
        sc = jnp.where(causal(), nt(qh, kf[:, cols(h)]), 0.0).astype(bf16)
        scores[h] = sc
        att[:, cols(h)] = nn(sc, v_ref[:, cols(h)])

    for h in range(HEADS):
        intra(h)
    serve_b(0)
    serve_a0()
    b_relay(0)
    scan = scan_total(0, scan, False)
    serve_b(1)
    b_relay(1)
    b_relay(-1)
    serve_a(0)
    p_top.wait_recv()
    f_top = cot(down_y, top, 1)
    m_bottom.wait_recv()
    f_bottom = cot(up_y, bottom, -1)
    scan = scan_back(0, scan, False)
    serve_b(2)
    b_relay(2)
    b_relay(-2)
    serve_a(1)
    share_w(0)
    serve_b(3)
    b_relay(3)
    b_relay(-3)
    scan = scan_share(0, scan)
    serve_a(2)
    share_w(1)
    share_w(-1)
    scan_end(0, scan, False)

    for h in range(HEADS):
        st = state[rows(h), :].astype(bf16)
        a = att[:, cols(h)] + nn(qf[:, cols(h)], st)
        r = lax.rsqrt(jnp.mean(a * a, axis=-1, keepdims=True) + EPS)
        u = a * r
        unit[:, cols(h)] = u
        inv[:, cols(h)] = jnp.broadcast_to(r, (ROWS, HD))
        n = u.astype(bf16)
        normed[:, cols(h)] = n
        prior[rows(h), :] = st
        t = u.T.astype(bf16)
        ntsend[h // 2, pl.ds((h % 2) * HD, HD), :] = t
    nt_copy = send(ntsend.at[1 - c], ntsib, at(dc=1), "nt")
    ntown[...] = ntsend[c]
    m_top.wait_recv()
    cot_c[1] = cot_share(up_y)
    b_relay(4)
    share_w(2)
    share_w(-2)
    serve_a(3)
    p_bottom.wait_recv()
    cot_c[3] = cot_share(down_y)

    half_rows = HD // 2

    def products(j):
        b = lax.rem(y + j, NY)
        cot_c[j].wait_recv()
        p = nn(ntown[...], call[b]) + nn(ntsib[...], csib[b])
        for o in range(NZ):
            lanes = slice(o * HD, (o + 1) * HD)
            pz[j, o] = p[:HD, lanes]
            xsend[0, j, o] = p[HD : HD + half_rows, lanes].astype(bf16)
            xsend[1, j, o] = p[HD + half_rows :, lanes].astype(bf16)

    rm, ro = ([], []), ([], [])
    groups = ((0, 1), (3, 2))

    def ring(g, i):
        if i:
            rm[g][i - 1].wait_recv()
        far = zat(s * (4 - i))
        for n, j in enumerate(groups[g]):
            p = pz[j, far]
            if i:
                p = p + rrecv[g, i - 1, n].astype(f32)
            rsend[g, i, n] = p.astype(bf16)
        rm[g].append(send(rsend.at[g, i], rrecv.at[g, i], at(dz=s), "ring"))
        if i < 3:
            if i:
                ro[g][i - 1].wait_recv()
            far = zat(-s * (3 - i))
            for n, j in enumerate(groups[g]):
                p = pz[j, far]
                if i:
                    p = p + rrecv[g, 4 + i - 1, n].astype(f32)
                rsend[g, 4 + i, n] = p.astype(bf16)
            ro[g].append(send(rsend.at[g, 4 + i], rrecv.at[g, 4 + i], at(dz=-s), "ring"))

    def ring_end(g):
        rm[g][3].wait_recv()
        ro[g][2].wait_recv()
        for n, j in enumerate(groups[g]):
            t = pz[j, z] + rrecv[g, 3, n].astype(f32) + rrecv[g, 6, n].astype(f32)
            zown[j] = t
            esend[j] = t.astype(bf16)

    def place_of(dx):
        return lax.rem(x + dx - y + 2 * NX, NX)

    def x_send(g):
        landed = arrival()
        for j in (2, 1, 3):
            send(xsend.at[g, place_of(j)], xrecv.at[g, j - 1], at(dx=j), "x", landed)
        return landed

    def x_sum(g, landed):
        await_all(xrecv.at[g], landed)
        for o in range(NZ):
            t = xsend[g, place_of(0), o].astype(f32)
            for j in range(NX - 1):
                t = t + xrecv[g, j, o].astype(f32)
            xsum[g, o] = t
            dsend[g, o] = t.astype(bf16)
        landed = arrival()
        for j in range(1, NZ):
            send(dsend.at[g, zat(j)], drecv.at[g, j - 1], at(dz=j), "d", landed)
        return landed

    nt_copy.wait_recv()
    products(0)
    products(1)
    ring(0, 0)
    products(3)
    share_w(3)
    share_w(-3)
    share_w(4)

    f_top.wait_recv()
    f_bottom.wait_recv()
    cot_c[2] = cot_share(far_y)
    products(2)
    ring(1, 0)
    x0 = x_send(0)
    x1 = x_send(1)

    def weight(b):
        return wall[b].reshape(FEATS, WIDTH)

    await_all(wall.at[pl.ds(0, 2)], wsib)
    lsend[2] = nt(normed[...], weight(far_y)).astype(bf16)
    l_far = [
        send(lsend.at[2, top], lfar.at[0], at(dy=1), "layer"),
        send(lsend.at[2, bottom], lfar.at[1], at(dy=-1), "layer"),
    ]
    up = nn(call[0], weight(0))
    for b in range(1, NY):
        up = up + nn(call[b], weight(b))
    for h in range(HEADS):
        u = unit[:, cols(h)]
        d = up[:, h * HD : (h + 1) * HD]
        m = jnp.mean(d * u, axis=-1, keepdims=True)
        da = (inv[:, cols(h)] * (d - u * m)).astype(bf16)
        datt[:, cols(h)] = da
        state[rows(h), :] = tn(qf[:, cols(h)], da)
    scan = scan_begin(1)
    near = arrival()
    lout[0] = nt(normed[...], weight(up_y))
    lsend[0, bottom] = lout[0, bottom].astype(bf16)
    send(lsend.at[0, bottom], lrecv.at[0, bottom], at(dy=1), "layer", near)
    lout[1] = nt(normed[...], weight(down_y))
    lsend[1, top] = lout[1, top].astype(bf16)
    send(lsend.at[1, top], lrecv.at[1, top], at(dy=-1), "layer", near)

    def layer_pass():
        l_far[0].wait_recv()
        lsend[0, top] = (lout[0, top] + lfar[0].astype(f32)).astype(bf16)
        send(lsend.at[0, top], lrecv.at[0, top], at(dy=1), "layer", near)
        l_far[1].wait_recv()
        lsend[1, bottom] = (lout[1, bottom] + lfar[1].astype(f32)).astype(bf16)
        send(lsend.at[1, bottom], lrecv.at[1, bottom], at(dy=-1), "layer", near)
        lout[2] = nt(normed[...], weight(y))

    ring(0, 1)
    scan = scan_chip(1, scan)

    def grads(h):
        da = datt[:, cols(h)]
        vh = v_ref[:, cols(h)]
        ds = jnp.where(causal(), nt(da, vh), 0.0).astype(bf16)
        qg = nn(ds, kf[:, cols(h)]) + nt(da, prior[rows(h), :])
        qg_ref[:, cols(h)] = (qg * slope(q_ref, h)).astype(bf16)
        kacc[:, cols(h)] = tn(ds, qf[:, cols(h)])
        vacc[:, cols(h)] = tn(scores[h], da)

    ring(1, 1)
    ring(0, 2)
    for h in range(HEADS):
        grads(h)
    scan = scan_total(1, scan, True)
    ring(1, 2)
    layer_pass()
    ring(0, 3)
    d0 = x_sum(0, x0)
    ring(1, 3)
    scan = scan_back(1, scan, True)
    ring_end(0)
    d1 = x_sum(1, x1)
    ring_end(1)
    landed_e = arrival()
    for j in range(1, NX):
        send(esend.at[place_of(j)], erecv.at[j - 1], at(dx=j), "e", landed_e)
    scan = scan_share(1, scan)
    scan_end(1, scan, True)
    for h in range(HEADS):
        st = state[rows(h), :].astype(bf16)
        kg = kacc[:, cols(h)] + nt(v_ref[:, cols(h)], st)
        kg_ref[:, cols(h)] = (kg * slope(k_ref, h)).astype(bf16)
        vg_ref[:, cols(h)] = (vacc[:, cols(h)] + nn(kf[:, cols(h)], st)).astype(bf16)

    await_all(lrecv, near)
    lo_ref[...] = (lout[2] + lrecv[0].astype(f32) + lrecv[1].astype(f32)).astype(bf16)

    await_all(erecv, landed_e)
    t = zown[place_of(0)]
    for j in range(NX - 1):
        t = t + erecv[j].astype(f32)
    mine[:, pl.ds(0, HD)] = t.T
    for g, landed in enumerate((d0, d1)):
        await_all(drecv.at[g], landed)
        t = xsum[g, z]
        for j in range(NZ - 1):
            t = t + drecv[g, j].astype(f32)
        xsum[g, z] = t
    mine[:, pl.ds(HD, HD)] = jnp.concatenate([xsum[0, z], xsum[1, z]], axis=0).T
    other = pl.multiple_of((1 - c) * WROWS, WROWS)
    last = send(mine.at[pl.ds(other, WROWS)], tsib_recv, at(dc=1), "last")
    last.wait_recv()
    here = mine[pl.ds(pl.multiple_of(c * WROWS, WROWS), WROWS), :] * grad_scale
    there = tsib_recv[...] * grad_scale
    dw_ref[:, pl.ds(0, 2 * HD)] = jnp.where(c == 0, here, there)
    dw_ref[:, pl.ds(2 * HD, 2 * HD)] = jnp.where(c == 0, there, here)
    sent("own", own_b)
    sent("chip", zrecv.at[:, pl.ds(0, NZ - 1)])
    sent("total", trecv.at[:, pl.ds(0, NX - 1)])
    sent("back", psend.at[:, pl.ds(0, NZ - 1)])
    sent("share", pre.at[:, pl.ds(0, half)])
    sent("xa", wall.at[pl.ds(0, NX - 1), 0, 0, part_a])
    sent("b", wall.at[0, pl.ds(0, NZ - 1), 0, part_b])
    sent("bx", wall.at[pl.ds(0, 2), :, 0, part_b])
    sent("br", wall.at[0, :, 0, part_b])
    sent("a", wall.at[:, pl.ds(0, NZ - 1), 0, part_a])
    sent("wshare", wall.at[pl.ds(0, 2)])
    sent("cot", call.at[pl.ds(0, 3)])
    sent("cot2", call)
    sent("nt", ntsib)
    sent("layer", lsend)
    sent("ring", rsend)
    sent("x", xrecv)
    sent("d", drecv)
    sent("e", erecv)
    sent("last", tsib_recv)
    assert not kinds and len(arrivals) == ARRIVALS


def write_out(*refs):
    sem = refs[-1]
    copies = [pltpu.make_async_copy(refs[i], refs[5 + i], sem.at[i]) for i in range(5)]
    for copy in copies:
        copy.start()
    for copy in copies:
        copy.wait()


def solution(mesh):
    split = Mesh(mesh.devices.reshape(NX, NZ, NC, NY), (*SEQ, "head"))
    placed = P(SEQ, "head")

    def shards(q, k, v, w, cot):
        shape = jax.ShapeDtypeStruct
        vm = pltpu.VMEM
        found = pl.pallas_call(
            functools.partial(kernel, 16384.0**-0.5),
            out_shape=(
                shape((ROWS, FEATS), bf16),
                shape((ROWS, WIDTH), bf16),
                shape((ROWS, WIDTH), bf16),
                shape((ROWS, WIDTH), bf16),
                shape((WROWS, WIDTH), f32),
            ),
            in_specs=[pl.BlockSpec(memory_space=pltpu.HBM)] * 5,
            out_specs=[pl.BlockSpec(memory_space=pltpu.VMEM)] * 5,
            scratch_shapes=[
                vm((ROWS, WIDTH), bf16),
                vm((ROWS, WIDTH), bf16),
                vm((ROWS, WIDTH), bf16),
                vm((ROWS, WIDTH), bf16),
                vm((ROWS, WIDTH), bf16),
                vm((HEADS, ROWS, ROWS), bf16),
                vm((ROWS, WIDTH), f32),
                vm((ROWS, WIDTH), f32),
                vm((ROWS, WIDTH), f32),
                vm((ROWS, WIDTH), bf16),
                vm((ROWS, WIDTH), bf16),
                vm((WIDTH, HD), bf16),
                vm((ROWS, WIDTH), f32),
                vm((ROWS, WIDTH), f32),
                vm((WIDTH, HD), f32),
                vm((2, WIDTH, HD), bf16),
                vm((2, WIDTH, HD), bf16),
                vm((2, 2 * HD, HD), bf16),
                vm((2, NZ, 2 * HD // NZ, HD), bf16),
                vm((2, 2 * HD // NZ, HD), bf16),
                vm((2, NX, 2 * HD // NZ, HD), bf16),
                vm((2, NZ, 2 * HD // NZ, HD), bf16),
                vm((2, WIDTH, HD), bf16),
                vm((NX, NZ, NC, WROWS, WIDTH), bf16),
                vm((NY, ROWS, FEATS), bf16),
                vm((NY, ROWS, FEATS), bf16),
                vm((3, ROWS, FEATS), f32),
                vm((3, ROWS, FEATS), bf16),
                vm((2, ROWS, FEATS), bf16),
                vm((2, ROWS // 2, FEATS), bf16),
                vm((2 * HD, ROWS), bf16),
                vm((2, 2 * HD, ROWS), bf16),
                vm((2 * HD, ROWS), bf16),
                vm((NX, NZ, HD, HD), f32),
                vm((2, NX, NZ, HD // 2, HD), bf16),
                vm((2, NX - 1, NZ, HD // 2, HD), bf16),
                vm((2, NZ, HD // 2, HD), f32),
                vm((2, NZ, HD // 2, HD), bf16),
                vm((2, NZ - 1, HD // 2, HD), bf16),
                vm((2, 7, 2, HD, HD), bf16),
                vm((2, 7, 2, HD, HD), bf16),
                vm((NX, HD, HD), f32),
                vm((NX, HD, HD), bf16),
                vm((NX - 1, HD, HD), bf16),
                vm((HD, 2 * HD), f32),
                vm((WROWS, 2 * HD), f32),
                pltpu.SemaphoreType.DMA((DEPARTURES,)),
                pltpu.SemaphoreType.DMA((ARRIVALS,)),
                pltpu.SemaphoreType.DMA((5,)),
            ],
            compiler_params=pltpu.CompilerParams(
                collective_id=0, has_side_effects=True, vmem_limit_bytes=56 * 2**20
            ),
            name="layer_step",
        )(q, k, v, w, cot)
        return pl.pallas_call(
            write_out,
            out_shape=[shape(a.shape, a.dtype) for a in found],
            in_specs=[pl.BlockSpec(memory_space=pltpu.VMEM)] * 5,
            out_specs=[pl.BlockSpec(memory_space=pltpu.HBM)] * 5,
            scratch_shapes=[pltpu.SemaphoreType.DMA((5,))],
            name="write_out",
        )(*found)

    return jax.shard_map(
        shards, mesh=split, in_specs=(placed,) * 5, out_specs=(placed,) * 5, check_vma=False
    )
```

```python
import functools

import jax
import jax.numpy as jnp
from jax import lax
from jax.experimental import pallas as pl
from jax.experimental.pallas import tpu as pltpu
from jax.sharding import Mesh
from jax.sharding import PartitionSpec as P

SEQ = ("seq_0", "seq_1", "seq_2")
NX, NZ, NC, NY = 4, 8, 2, 4
HD = 128
HEADS = 4
ROWS = 256
WIDTH = HEADS * HD
FEATS = 1024
EPS = 1e-06
WROWS = 64
WA = 16
PARTS = 4
ARRIVALS = 95
DEPARTURES = 20
MESH = pl.DeviceIdType.MESH
f32 = jnp.float32
bf16 = jnp.bfloat16


def nn(a, b):
    return lax.dot_general(a, b, (((1,), (0,)), ((), ())), preferred_element_type=f32)


def nt(a, b):
    return lax.dot_general(a, b, (((1,), (1,)), ((), ())), preferred_element_type=f32)


def tn(a, b):
    return lax.dot_general(a, b, (((0,), (0,)), ((), ())), preferred_element_type=f32)


def kernel(
    grad_scale,
    q_hbm, k_hbm, v_hbm, w_hbm, c_hbm,
    lo_hbm, qg_hbm, kg_hbm, vg_hbm, dw_hbm,
    lo_ref, qg_ref, kg_ref, vg_ref, dw_ref,
    q_ref, k_ref, v_ref, qf, kf, scores, att, unit, inv, normed, datt, prior, kacc, vacc,
    state, own_b, sib_b, zsend, zrecv, tsend, trecv, psend, pre,
    wall, call, csib, lout, lsend, lrecv, lfar, ntown, ntsend, ntsib,
    pz, xsend, xrecv, xsum, dsend, drecv, rsend, rrecv, zown, esend, erecv, mine, tsib_recv,
    ssem, rsem, lsem,
):
    x, z, c, y = (lax.axis_index(a) for a in (*SEQ, "head"))
    s = 1 - 2 * c

    def at(dx=0, dz=0, dc=0, dy=0):
        return (
            lax.rem(x + dx + NX, NX),
            lax.rem(z + dz + NZ, NZ),
            lax.rem(c + dc, NC),
            lax.rem(y + dy + NY, NY),
        )

    def zat(offset):
        return lax.rem(z + offset + 2 * NZ, NZ)

    peers = [at(dc=1)]
    peers += [at(dz=j) for j in range(1, NZ)]
    peers += [at(dx=j) for j in range(1, NX)]
    peers += [at(dy=j) for j in range(1, NY)]

    kinds = {}
    arrivals = []

    def arrival():
        arrivals.append(None)
        return rsem.at[len(arrivals) - 1]

    def send(src, dst, device, kind, landed=None):
        copy = pltpu.make_async_remote_copy(
            src_ref=src, dst_ref=dst, send_sem=ssem.at[kinds.setdefault(kind, len(kinds))],
            recv_sem=arrival() if landed is None else landed,
            device_id=device, device_id_type=MESH,
        )
        copy.start()
        return copy

    def await_all(ref, sem):
        pltpu.make_async_copy(ref, ref, sem).wait()

    def sent(kind, ref):
        await_all(ref, ssem.at[kinds.pop(kind)])

    def cols(h):
        return pl.ds(h * HD, HD)

    def rows(h):
        return pl.ds(h * HD, HD)

    def phi(ref, h):
        a = ref[:, cols(h)].astype(f32)
        return jnp.where(a > 0, a + 1.0, jnp.exp(jnp.minimum(a, 0.0)))

    def slope(ref, h):
        a = ref[:, cols(h)].astype(f32)
        return jnp.where(a > 0, 1.0, jnp.exp(jnp.minimum(a, 0.0)))

    def causal():
        t = lax.broadcasted_iota(jnp.int32, (ROWS, ROWS), 0)
        u = lax.broadcasted_iota(jnp.int32, (ROWS, ROWS), 1)
        return u <= t

    half = 2 * HD
    piece = half // NZ
    lo_row = pl.multiple_of(half * c, half)

    def scan_begin(i):
        own_b[i] = state[...].astype(bf16)
        return send(own_b.at[i], sib_b.at[i], at(dc=1), "own")

    def scan_chip(i, copy):
        copy.wait_recv()
        total = own_b[i, pl.ds(lo_row, half)].astype(f32) + sib_b[i, pl.ds(lo_row, half)].astype(f32)
        zsend[i] = total.astype(bf16)
        landed = arrival()
        for j in range(1, NZ):
            rows_of = pl.ds(pl.multiple_of(zat(j) * piece, piece), piece)
            send(zsend.at[i, rows_of], zrecv.at[i, z], at(dz=j), "chip", landed)
        return landed

    def scan_total(i, landed, reverse):
        await_all(zrecv.at[i, pl.ds(0, NZ - 1)], landed)
        zrecv[i, z] = zsend[i, pl.ds(pl.multiple_of(z * piece, piece), piece)]
        running = jnp.zeros((piece, HD), f32)
        inner = [None] * NZ
        for o in reversed(range(NZ)) if reverse else range(NZ):
            inner[o] = running
            running = running + zrecv[i, o].astype(f32)
        tsend[i] = running.astype(bf16)
        landed = arrival()
        for j in range(1, NX):
            send(tsend.at[i], trecv.at[i, x], at(dx=j), "total", landed)
        return inner, landed

    def scan_back(i, state_in, reverse):
        inner, landed = state_in
        await_all(trecv.at[i, pl.ds(0, NX - 1)], landed)
        trecv[i, x] = tsend[i]
        outer = jnp.zeros((piece, HD), f32)
        for o in range(NX):
            passed = (o > x) if reverse else (o < x)
            outer = outer + jnp.where(passed, trecv[i, o].astype(f32), 0.0)
        for o in range(NZ):
            psend[i, o] = (inner[o] + outer).astype(bf16)
        place = pl.ds(pl.multiple_of(half * c + piece * z, piece), piece)
        landed = arrival()
        for j in range(1, NZ):
            send(psend.at[i, zat(j)], pre.at[i, place], at(dz=j), "back", landed)
        pre[i, place] = psend[i, z]
        return landed

    def scan_share(i, landed):
        await_all(psend.at[i, pl.ds(0, NZ - 1)], landed)
        return send(pre.at[i, pl.ds(lo_row, half)], pre.at[i, pl.ds(lo_row, half)], at(dc=1), "share")

    def scan_end(i, copy, reverse):
        copy.wait_recv()
        takes = (c == 0) if reverse else (c == 1)
        state[...] = pre[i].astype(f32) + jnp.where(takes, sib_b[i].astype(f32), 0.0)

    barrier = pltpu.get_barrier_semaphore()
    for peer in peers:
        pl.semaphore_signal(barrier, inc=1, device_id=peer, device_id_type=MESH)
    def load(i, src, dst):
        copy = pltpu.make_async_copy(src, dst, lsem.at[i])
        copy.start()
        return copy

    k_in = load(0, k_hbm, k_ref)
    v_in = load(1, v_hbm, v_ref)
    w_in = load(2, w_hbm, wall.at[x, z, c])
    c_in = load(3, c_hbm, call.at[y])
    q_in = load(4, q_hbm, q_ref)
    k_in.wait()
    v_in.wait()
    for h in range(HEADS):
        kh = phi(k_ref, h).astype(bf16)
        kf[:, cols(h)] = kh
        state[rows(h), :] = tn(kh, v_ref[:, cols(h)])
    for copy in (w_in, c_in, q_in):
        copy.wait()
    pl.semaphore_wait(barrier, len(peers))

    scan = scan_begin(0)
    part_a = pl.ds(0, WA)
    part_b = pl.ds(WA, WROWS - WA)
    xa = arrival()
    for j in range(1, NX):
        send(wall.at[x, z, c, part_a], wall.at[x, z, c, part_a], at(dx=j), "xa", xa)
    left, right = pl.ds(0, 2 * HD), pl.ds(2 * HD, 2 * HD)
    left_x, right_x = lax.rem(x + NX - 1, NX), lax.rem(x + 1, NX)

    def place(k):
        return zat(-s * k)

    def b_across(k):
        block = wall.at[x, place(k), c, part_b]
        return send(block, block, at(dx=1), "bx"), send(block, block, at(dx=-1), "bx")

    def b_relay(k):
        up_copy, down_copy = xb[k]
        landed = arrival()
        up_copy.wait_recv()
        block = wall.at[left_x, place(k), c, part_b, left]
        send(block, block, at(dx=1), "br", landed)
        down_copy.wait_recv()
        block = wall.at[right_x, place(k), c, part_b, right]
        send(block, block, at(dx=-1), "br", landed)
        xr[k] = landed

    def b_step(origin, way):
        block = wall.at[x, origin, c, part_b]
        return send(block, block, at(dz=way), "b")

    def a_step(g, origin, way):
        group = wall.at[pl.ds(2 * g, 2), origin, c, part_a]
        return send(group, group, at(dz=way), "a")

    bm = [b_step(z, s)]
    bo = [b_step(z, -s)]
    top, bottom = pl.ds(0, ROWS // 2), pl.ds(ROWS // 2, ROWS // 2)
    up_y, down_y = lax.rem(y + 1, NY), lax.rem(y + NY - 1, NY)
    far_y = lax.rem(y + 2, NY)

    def cot(b, part, way):
        return send(call.at[b, part], call.at[b, part], at(dy=way), "cot")

    p_top = cot(y, top, 1)
    m_bottom = cot(y, bottom, -1)
    p_bottom = cot(y, bottom, 1)
    m_top = cot(y, top, -1)
    xb, xr = {0: b_across(0)}, {}
    scan = scan_chip(0, scan)

    def cot_share(b):
        return send(call.at[b], csib.at[b], at(dc=1), "cot2")

    cot_c = {0: cot_share(y)}
    am, ao = ([], []), ([], [])

    def serve_b(i):
        bm[i].wait_recv()
        if i < 3:
            bm.append(b_step(place(i + 1), s))
            bo[i].wait_recv()
            if i < 2:
                bo.append(b_step(place(-i - 1), -s))
            xb[-i - 1] = b_across(-i - 1)
        xb[i + 1] = b_across(i + 1)

    def serve_a0():
        await_all(wall.at[pl.ds(0, NX - 1), 0, 0, part_a], xa)
        for g in (0, 1):
            am[g].append(a_step(g, z, s))
            ao[g].append(a_step(g, z, -s))

    def serve_a(i):
        for g in (0, 1):
            am[g][i].wait_recv()
            if i < 3:
                am[g].append(a_step(g, place(i + 1), s))
                ao[g][i].wait_recv()
                if i < 2:
                    ao[g].append(a_step(g, place(-i - 1), -s))

    wsib = arrival()

    def share_b(k):
        await_all(wall.at[0, 0, 0, part_b], xr[k])
        group = wall.at[:, place(k), c, part_b]
        send(group, group, at(dc=1), "wshare", wsib)

    def share_a():
        group = wall.at[:, :, c, part_a]
        send(group, group, at(dc=1), "wshare", wsib)

    def intra(h):
        qh = phi(q_ref, h).astype(bf16)
        qf[:, cols(h)] = qh
        sc = jnp.where(causal(), nt(qh, kf[:, cols(h)]), 0.0).astype(bf16)
        scores[h] = sc
        att[:, cols(h)] = nn(sc, v_ref[:, cols(h)])

    for h in range(HEADS):
        intra(h)
    serve_b(0)
    serve_a0()
    b_relay(0)
    scan = scan_total(0, scan, False)
    serve_b(1)
    serve_a(0)
    b_relay(1)
    b_relay(-1)
    p_top.wait_recv()
    f_top = cot(down_y, top, 1)
    m_bottom.wait_recv()
    f_bottom = cot(up_y, bottom, -1)
    scan = scan_back(0, scan, False)
    serve_b(2)
    serve_a(1)
    b_relay(2)
    b_relay(-2)
    share_b(0)
    serve_b(3)
    serve_a(2)
    m_top.wait_recv()
    cot_c[1] = cot_share(up_y)
    b_relay(3)
    b_relay(-3)
    share_b(1)
    share_b(-1)
    scan = scan_share(0, scan)
    p_bottom.wait_recv()
    cot_c[3] = cot_share(down_y)
    b_relay(4)
    scan_end(0, scan, False)

    for h in range(HEADS):
        st = state[rows(h), :].astype(bf16)
        a = att[:, cols(h)] + nn(qf[:, cols(h)], st)
        r = lax.rsqrt(jnp.mean(a * a, axis=-1, keepdims=True) + EPS)
        u = a * r
        unit[:, cols(h)] = u
        inv[:, cols(h)] = jnp.broadcast_to(r, (ROWS, HD))
        n = u.astype(bf16)
        normed[:, cols(h)] = n
        prior[rows(h), :] = st
        t = u.T.astype(bf16)
        ntsend[h // 2, pl.ds((h % 2) * HD, HD), :] = t
    nt_copy = send(ntsend.at[1 - c], ntsib, at(dc=1), "nt")
    ntown[...] = ntsend[c]
    share_b(2)
    share_b(-2)
    serve_a(3)
    share_a()

    part_rows = HD // PARTS

    def products(j):
        b = lax.rem(y + j, NY)
        cot_c[j].wait_recv()
        p = nn(ntown[...], call[b]) + nn(ntsib[...], csib[b])
        for o in range(NZ):
            lanes = slice(o * HD, (o + 1) * HD)
            pz[j, o] = p[:HD, lanes]
            for g in range(PARTS):
                low = HD + g * part_rows
                xsend[g, j, o] = p[low : low + part_rows, lanes].astype(bf16)

    rm, ro = ([], []), ([], [])
    groups = ((0, 1, 3), (2,))

    def ring_send(g, i, way):
        count = pl.ds(0, len(groups[g]))
        return send(rsend.at[g, i, count], rrecv.at[g, i, count], at(dz=way), "ring")

    def ring(g, i):
        if i:
            rm[g][i - 1].wait_recv()
        far = zat(s * (4 - i))
        for n, j in enumerate(groups[g]):
            p = pz[j, far]
            if i:
                p = p + rrecv[g, i - 1, n].astype(f32)
            rsend[g, i, n] = p.astype(bf16)
        rm[g].append(ring_send(g, i, s))
        if i < 3:
            if i:
                ro[g][i - 1].wait_recv()
            far = zat(-s * (3 - i))
            for n, j in enumerate(groups[g]):
                p = pz[j, far]
                if i:
                    p = p + rrecv[g, 4 + i - 1, n].astype(f32)
                rsend[g, 4 + i, n] = p.astype(bf16)
            ro[g].append(ring_send(g, 4 + i, -s))

    def ring_end(g):
        rm[g][3].wait_recv()
        ro[g][2].wait_recv()
        for n, j in enumerate(groups[g]):
            t = pz[j, z] + rrecv[g, 3, n].astype(f32) + rrecv[g, 6, n].astype(f32)
            zown[j] = t
            esend[j] = t.astype(bf16)

    def place_of(dx):
        return lax.rem(x + dx - y + 2 * NX, NX)

    def x_send(g):
        landed = arrival()
        for j in (2, 1, 3):
            send(xsend.at[g, place_of(j)], xrecv.at[g, j - 1], at(dx=j), "x", landed)
        return landed

    def x_sum(g, landed):
        await_all(xrecv.at[g], landed)
        for o in range(NZ):
            t = xsend[g, place_of(0), o].astype(f32)
            for j in range(NX - 1):
                t = t + xrecv[g, j, o].astype(f32)
            xsum[g, o] = t
            dsend[g, o] = t.astype(bf16)
        landed = arrival()
        for j in range(1, NZ):
            send(dsend.at[g, zat(j)], drecv.at[g, j - 1], at(dz=j), "d", landed)
        return landed

    nt_copy.wait_recv()
    products(0)
    products(1)
    products(3)
    ring(0, 0)
    f_top.wait_recv()
    f_bottom.wait_recv()
    cot_c[2] = cot_share(far_y)
    share_b(3)
    share_b(-3)
    share_b(4)
    products(2)
    xs = [x_send(0)]
    ring(1, 0)
    xs += [x_send(g) for g in range(1, PARTS)]

    def weight(b):
        return wall[b].reshape(FEATS, WIDTH)

    await_all(wall.at[pl.ds(0, 2)], wsib)
    lsend[2] = nt(normed[...], weight(far_y)).astype(bf16)
    l_far = [
        send(lsend.at[2, top], lfar.at[0], at(dy=1), "layer"),
        send(lsend.at[2, bottom], lfar.at[1], at(dy=-1), "layer"),
    ]
    up = nn(call[0], weight(0))
    for b in range(1, NY):
        up = up + nn(call[b], weight(b))
    for h in range(HEADS):
        u = unit[:, cols(h)]
        d = up[:, h * HD : (h + 1) * HD]
        m = jnp.mean(d * u, axis=-1, keepdims=True)
        da = (inv[:, cols(h)] * (d - u * m)).astype(bf16)
        datt[:, cols(h)] = da
        state[rows(h), :] = tn(qf[:, cols(h)], da)
    scan = scan_begin(1)
    near = arrival()
    lout[0] = nt(normed[...], weight(up_y))
    lsend[0, bottom] = lout[0, bottom].astype(bf16)
    send(lsend.at[0, bottom], lrecv.at[0, bottom], at(dy=1), "layer", near)
    lout[1] = nt(normed[...], weight(down_y))
    lsend[1, top] = lout[1, top].astype(bf16)
    send(lsend.at[1, top], lrecv.at[1, top], at(dy=-1), "layer", near)

    def layer_pass():
        l_far[0].wait_recv()
        lsend[0, top] = (lout[0, top] + lfar[0].astype(f32)).astype(bf16)
        send(lsend.at[0, top], lrecv.at[0, top], at(dy=1), "layer", near)
        l_far[1].wait_recv()
        lsend[1, bottom] = (lout[1, bottom] + lfar[1].astype(f32)).astype(bf16)
        send(lsend.at[1, bottom], lrecv.at[1, bottom], at(dy=-1), "layer", near)
        lout[2] = nt(normed[...], weight(y))

    ring(0, 1)
    scan = scan_chip(1, scan)

    def grads(h):
        da = datt[:, cols(h)]
        vh = v_ref[:, cols(h)]
        ds = jnp.where(causal(), nt(da, vh), 0.0).astype(bf16)
        qg = nn(ds, kf[:, cols(h)]) + nt(da, prior[rows(h), :])
        qg_ref[:, cols(h)] = (qg * slope(q_ref, h)).astype(bf16)
        kacc[:, cols(h)] = tn(ds, qf[:, cols(h)])
        vacc[:, cols(h)] = tn(scores[h], da)

    ring(1, 1)
    ring(0, 2)
    for h in range(HEADS):
        grads(h)
    outs = [load(0, qg_ref, qg_hbm)]
    ds = [x_sum(0, xs[0])]
    ring(1, 2)
    scan = scan_total(1, scan, True)
    ring(0, 3)
    ds.append(x_sum(1, xs[1]))
    layer_pass()
    ring(1, 3)
    ds.append(x_sum(2, xs[2]))
    scan = scan_back(1, scan, True)
    ring_end(0)
    ring_end(1)
    landed_e = arrival()
    for j in range(1, NX):
        send(esend.at[place_of(j)], erecv.at[j - 1], at(dx=j), "e", landed_e)
    ds.append(x_sum(3, xs[3]))
    scan = scan_share(1, scan)
    await_all(erecv, landed_e)
    t = zown[place_of(0)]
    for j in range(NX - 1):
        t = t + erecv[j].astype(f32)
    mine[:, pl.ds(0, HD)] = t.T
    for g, landed in enumerate(ds):
        await_all(drecv.at[g], landed)
        t = xsum[g, z]
        for j in range(NZ - 1):
            t = t + drecv[g, j].astype(f32)
        xsum[g, z] = t
    mine[:, pl.ds(HD, HD)] = jnp.concatenate([xsum[g, z] for g in range(PARTS)], axis=0).T
    other = pl.multiple_of((1 - c) * WROWS, WROWS)
    last = send(mine.at[pl.ds(other, WROWS)], tsib_recv, at(dc=1), "last")
    scan_end(1, scan, True)
    for h in range(HEADS):
        st = state[rows(h), :].astype(bf16)
        kg = kacc[:, cols(h)] + nt(v_ref[:, cols(h)], st)
        kg_ref[:, cols(h)] = (kg * slope(k_ref, h)).astype(bf16)
        vg_ref[:, cols(h)] = (vacc[:, cols(h)] + nn(kf[:, cols(h)], st)).astype(bf16)

    outs += [load(1, kg_ref, kg_hbm), load(2, vg_ref, vg_hbm)]
    await_all(lrecv, near)
    lo_ref[...] = (lout[2] + lrecv[0].astype(f32) + lrecv[1].astype(f32)).astype(bf16)

    outs.append(load(3, lo_ref, lo_hbm))
    last.wait_recv()
    here = mine[pl.ds(pl.multiple_of(c * WROWS, WROWS), WROWS), :] * grad_scale
    there = tsib_recv[...] * grad_scale
    dw_ref[:, pl.ds(0, 2 * HD)] = jnp.where(c == 0, here, there)
    dw_ref[:, pl.ds(2 * HD, 2 * HD)] = jnp.where(c == 0, there, here)
    outs.append(load(4, dw_ref, dw_hbm))
    sent("own", own_b)
    sent("chip", zrecv.at[:, pl.ds(0, NZ - 1)])
    sent("total", trecv.at[:, pl.ds(0, NX - 1)])
    sent("back", psend.at[:, pl.ds(0, NZ - 1)])
    sent("share", pre.at[:, pl.ds(0, half)])
    sent("xa", wall.at[pl.ds(0, NX - 1), 0, 0, part_a])
    sent("b", wall.at[0, pl.ds(0, NZ - 1), 0, part_b])
    sent("bx", wall.at[pl.ds(0, 2), :, 0, part_b])
    sent("br", wall.at[0, :, 0, part_b])
    sent("a", wall.at[:, pl.ds(0, NZ - 1), 0, part_a])
    sent("wshare", wall.at[pl.ds(0, 2)])
    sent("cot", call.at[pl.ds(0, 3)])
    sent("cot2", call)
    sent("nt", ntsib)
    sent("layer", lsend)
    sent("ring", rsend.at[:, :, pl.ds(0, 2)])
    sent("x", xrecv)
    sent("d", drecv)
    sent("e", erecv)
    sent("last", tsib_recv)
    for copy in outs:
        copy.wait()
    assert not kinds and len(arrivals) == ARRIVALS


def write_out(*refs):
    ins, outs, bufs, (here, there) = refs[:5], refs[5:10], refs[10:15], refs[15:]

    def start(i, src, dst, sem):
        copy = pltpu.make_async_copy(src, dst, sem.at[i])
        copy.start()
        return copy

    coming = [start(i, ins[i], bufs[i], here) for i in range(5)]
    going = []
    for i in (4, 1, 2, 3, 0):
        coming[i].wait()
        going.append(start(i, bufs[i], outs[i], there))
    for copy in going:
        copy.wait()


def solution(mesh):
    split = Mesh(mesh.devices.reshape(NX, NZ, NC, NY), (*SEQ, "head"))
    placed = P(SEQ, "head")

    def shards(q, k, v, w, cot):
        shape = jax.ShapeDtypeStruct
        vm = pltpu.VMEM
        found = pl.pallas_call(
            functools.partial(kernel, 16384.0**-0.5),
            out_shape=(
                shape((ROWS, FEATS), bf16),
                shape((ROWS, WIDTH), bf16),
                shape((ROWS, WIDTH), bf16),
                shape((ROWS, WIDTH), bf16),
                shape((WROWS, WIDTH), f32),
            ),
            in_specs=[pl.BlockSpec(memory_space=pltpu.HBM)] * 5,
            out_specs=[pl.BlockSpec(memory_space=pltpu.HBM)] * 5,
            scratch_shapes=[
                vm((ROWS, FEATS), bf16),
                vm((ROWS, WIDTH), bf16),
                vm((ROWS, WIDTH), bf16),
                vm((ROWS, WIDTH), bf16),
                vm((WROWS, WIDTH), f32),
                vm((ROWS, WIDTH), bf16),
                vm((ROWS, WIDTH), bf16),
                vm((ROWS, WIDTH), bf16),
                vm((ROWS, WIDTH), bf16),
                vm((ROWS, WIDTH), bf16),
                vm((HEADS, ROWS, ROWS), bf16),
                vm((ROWS, WIDTH), f32),
                vm((ROWS, WIDTH), f32),
                vm((ROWS, WIDTH), f32),
                vm((ROWS, WIDTH), bf16),
                vm((ROWS, WIDTH), bf16),
                vm((WIDTH, HD), bf16),
                vm((ROWS, WIDTH), f32),
                vm((ROWS, WIDTH), f32),
                vm((WIDTH, HD), f32),
                vm((2, WIDTH, HD), bf16),
                vm((2, WIDTH, HD), bf16),
                vm((2, 2 * HD, HD), bf16),
                vm((2, NZ, 2 * HD // NZ, HD), bf16),
                vm((2, 2 * HD // NZ, HD), bf16),
                vm((2, NX, 2 * HD // NZ, HD), bf16),
                vm((2, NZ, 2 * HD // NZ, HD), bf16),
                vm((2, WIDTH, HD), bf16),
                vm((NX, NZ, NC, WROWS, WIDTH), bf16),
                vm((NY, ROWS, FEATS), bf16),
                vm((NY, ROWS, FEATS), bf16),
                vm((3, ROWS, FEATS), f32),
                vm((3, ROWS, FEATS), bf16),
                vm((2, ROWS, FEATS), bf16),
                vm((2, ROWS // 2, FEATS), bf16),
                vm((2 * HD, ROWS), bf16),
                vm((2, 2 * HD, ROWS), bf16),
                vm((2 * HD, ROWS), bf16),
                vm((NX, NZ, HD, HD), f32),
                vm((PARTS, NX, NZ, HD // PARTS, HD), bf16),
                vm((PARTS, NX - 1, NZ, HD // PARTS, HD), bf16),
                vm((PARTS, NZ, HD // PARTS, HD), f32),
                vm((PARTS, NZ, HD // PARTS, HD), bf16),
                vm((PARTS, NZ - 1, HD // PARTS, HD), bf16),
                vm((2, 7, 3, HD, HD), bf16),
                vm((2, 7, 3, HD, HD), bf16),
                vm((NX, HD, HD), f32),
                vm((NX, HD, HD), bf16),
                vm((NX - 1, HD, HD), bf16),
                vm((HD, 2 * HD), f32),
                vm((WROWS, 2 * HD), f32),
                pltpu.SemaphoreType.DMA((DEPARTURES,)),
                pltpu.SemaphoreType.DMA((ARRIVALS,)),
                pltpu.SemaphoreType.DMA((5,)),
            ],
            compiler_params=pltpu.CompilerParams(
                collective_id=0, has_side_effects=True, vmem_limit_bytes=56 * 2**20
            ),
            name="layer_step",
        )(q, k, v, w, cot)
        return pl.pallas_call(
            write_out,
            out_shape=[shape(a.shape, a.dtype) for a in found],
            in_specs=[pl.BlockSpec(memory_space=pltpu.HBM)] * 5,
            out_specs=[pl.BlockSpec(memory_space=pltpu.HBM)] * 5,
            scratch_shapes=[
                *(vm(a.shape, a.dtype) for a in found),
                pltpu.SemaphoreType.DMA((5,)),
                pltpu.SemaphoreType.DMA((5,)),
            ],
            name="write_out",
        )(*found)

    return jax.shard_map(
        shards, mesh=split, in_specs=(placed,) * 5, out_specs=(placed,) * 5, check_vma=False
    )
```

```python
import functools

import jax
import jax.numpy as jnp
from jax import lax
from jax.experimental import pallas as pl
from jax.experimental.pallas import tpu as pltpu
from jax.sharding import Mesh
from jax.sharding import PartitionSpec as P

SEQ = ("seq_0", "seq_1", "seq_2")
NX, NZ, NC, NY = 4, 8, 2, 4
HD = 128
HEADS = 4
ROWS = 256
WIDTH = HEADS * HD
FEATS = 1024
EPS = 1e-06
WROWS = 64
WA = 16
PARTS = 4
ARRIVALS = 95
DEPARTURES = 20
MESH = pl.DeviceIdType.MESH
f32 = jnp.float32
bf16 = jnp.bfloat16


def nn(a, b):
    return lax.dot_general(a, b, (((1,), (0,)), ((), ())), preferred_element_type=f32)


def nt(a, b):
    return lax.dot_general(a, b, (((1,), (1,)), ((), ())), preferred_element_type=f32)


def tn(a, b):
    return lax.dot_general(a, b, (((0,), (0,)), ((), ())), preferred_element_type=f32)


def kernel(
    grad_scale,
    q_hbm, k_hbm, v_hbm, w_hbm, c_hbm,
    lo_hbm, qg_hbm, kg_hbm, vg_hbm, dw_hbm,
    lo_ref, qg_ref, kg_ref, vg_ref, dw_ref,
    q_ref, k_ref, v_ref, qf, kf, scores, att, unit, inv, normed, datt, prior, kacc, vacc,
    state, own_b, sib_b, zsend, zrecv, tsend, trecv, psend, pre,
    wall, call, csib, lout, lsend, lrecv, lfar, ntown, ntsend, ntsib,
    pz, xsend, xrecv, xsum, dsend, drecv, rsend, rrecv, zown, esend, erecv, mine, tsib_recv,
    ssem, rsem, lsem,
):
    x, z, c, y = (lax.axis_index(a) for a in (*SEQ, "head"))
    s = 1 - 2 * c

    def at(dx=0, dz=0, dc=0, dy=0):
        return (
            lax.rem(x + dx + NX, NX),
            lax.rem(z + dz + NZ, NZ),
            lax.rem(c + dc, NC),
            lax.rem(y + dy + NY, NY),
        )

    def zat(offset):
        return lax.rem(z + offset + 2 * NZ, NZ)

    peers = [at(dc=1)]
    peers += [at(dz=j) for j in range(1, NZ)]
    peers += [at(dx=j) for j in range(1, NX)]
    peers += [at(dy=j) for j in range(1, NY)]

    kinds = {}
    arrivals = []

    def arrival():
        arrivals.append(None)
        return rsem.at[len(arrivals) - 1]

    def send(src, dst, device, kind, landed=None):
        copy = pltpu.make_async_remote_copy(
            src_ref=src, dst_ref=dst, send_sem=ssem.at[kinds.setdefault(kind, len(kinds))],
            recv_sem=arrival() if landed is None else landed,
            device_id=device, device_id_type=MESH,
        )
        copy.start()
        return copy

    def await_all(ref, sem):
        pltpu.make_async_copy(ref, ref, sem).wait()

    def sent(kind, ref):
        await_all(ref, ssem.at[kinds.pop(kind)])

    def cols(h):
        return pl.ds(h * HD, HD)

    def rows(h):
        return pl.ds(h * HD, HD)

    def phi(ref, h):
        a = ref[:, cols(h)].astype(f32)
        return jnp.where(a > 0, a + 1.0, jnp.exp(jnp.minimum(a, 0.0)))

    def slope(ref, h):
        a = ref[:, cols(h)].astype(f32)
        return jnp.where(a > 0, 1.0, jnp.exp(jnp.minimum(a, 0.0)))

    def causal():
        t = lax.broadcasted_iota(jnp.int32, (ROWS, ROWS), 0)
        u = lax.broadcasted_iota(jnp.int32, (ROWS, ROWS), 1)
        return u <= t

    half = 2 * HD
    piece = half // NZ
    lo_row = pl.multiple_of(half * c, half)

    def scan_begin(i):
        own_b[i] = state[...].astype(bf16)
        return send(own_b.at[i], sib_b.at[i], at(dc=1), "own")

    def scan_chip(i, copy):
        copy.wait_recv()
        total = own_b[i, pl.ds(lo_row, half)].astype(f32) + sib_b[i, pl.ds(lo_row, half)].astype(f32)
        zsend[i] = total.astype(bf16)
        landed = arrival()
        for j in range(1, NZ):
            rows_of = pl.ds(pl.multiple_of(zat(j) * piece, piece), piece)
            send(zsend.at[i, rows_of], zrecv.at[i, z], at(dz=j), "chip", landed)
        return landed

    def scan_total(i, landed, reverse):
        await_all(zrecv.at[i, pl.ds(0, NZ - 1)], landed)
        zrecv[i, z] = zsend[i, pl.ds(pl.multiple_of(z * piece, piece), piece)]
        running = jnp.zeros((piece, HD), f32)
        inner = [None] * NZ
        for o in reversed(range(NZ)) if reverse else range(NZ):
            inner[o] = running
            running = running + zrecv[i, o].astype(f32)
        tsend[i] = running.astype(bf16)
        landed = arrival()
        for j in range(1, NX):
            send(tsend.at[i], trecv.at[i, x], at(dx=j), "total", landed)
        return inner, landed

    def scan_back(i, state_in, reverse):
        inner, landed = state_in
        await_all(trecv.at[i, pl.ds(0, NX - 1)], landed)
        trecv[i, x] = tsend[i]
        outer = jnp.zeros((piece, HD), f32)
        for o in range(NX):
            passed = (o > x) if reverse else (o < x)
            outer = outer + jnp.where(passed, trecv[i, o].astype(f32), 0.0)
        for o in range(NZ):
            psend[i, o] = (inner[o] + outer).astype(bf16)
        place = pl.ds(pl.multiple_of(half * c + piece * z, piece), piece)
        landed = arrival()
        for j in range(1, NZ):
            send(psend.at[i, zat(j)], pre.at[i, place], at(dz=j), "back", landed)
        pre[i, place] = psend[i, z]
        return landed

    def scan_share(i, landed):
        await_all(psend.at[i, pl.ds(0, NZ - 1)], landed)
        return send(pre.at[i, pl.ds(lo_row, half)], pre.at[i, pl.ds(lo_row, half)], at(dc=1), "share")

    def scan_end(i, copy, reverse):
        copy.wait_recv()
        takes = (c == 0) if reverse else (c == 1)
        state[...] = pre[i].astype(f32) + jnp.where(takes, sib_b[i].astype(f32), 0.0)

    barrier = pltpu.get_barrier_semaphore()
    for peer in peers:
        pl.semaphore_signal(barrier, inc=1, device_id=peer, device_id_type=MESH)
    def load(i, src, dst):
        copy = pltpu.make_async_copy(src, dst, lsem.at[i])
        copy.start()
        return copy

    k_in = load(0, k_hbm, k_ref)
    v_in = load(1, v_hbm, v_ref)
    w_in = load(2, w_hbm, wall.at[x, z, c])
    c_in = load(3, c_hbm, call.at[y])
    q_in = load(4, q_hbm, q_ref)
    k_in.wait()
    v_in.wait()
    for h in range(HEADS):
        kh = phi(k_ref, h).astype(bf16)
        kf[:, cols(h)] = kh
        state[rows(h), :] = tn(kh, v_ref[:, cols(h)])
    for copy in (w_in, c_in, q_in):
        copy.wait()
    pl.semaphore_wait(barrier, len(peers))

    scan = scan_begin(0)
    part_a = pl.ds(0, WA)
    part_b = pl.ds(WA, WROWS - WA)
    xa = arrival()
    for j in range(1, NX):
        send(wall.at[x, z, c, part_a], wall.at[x, z, c, part_a], at(dx=j), "xa", xa)
    left, right = pl.ds(0, 2 * HD), pl.ds(2 * HD, 2 * HD)
    left_x, right_x = lax.rem(x + NX - 1, NX), lax.rem(x + 1, NX)

    def place(k):
        return zat(-s * k)

    def b_across(k):
        block = wall.at[x, place(k), c, part_b]
        return send(block, block, at(dx=1), "bx"), send(block, block, at(dx=-1), "bx")

    def b_relay(k):
        up_copy, down_copy = xb[k]
        landed = arrival()
        up_copy.wait_recv()
        block = wall.at[left_x, place(k), c, part_b, left]
        send(block, block, at(dx=1), "br", landed)
        down_copy.wait_recv()
        block = wall.at[right_x, place(k), c, part_b, right]
        send(block, block, at(dx=-1), "br", landed)
        xr[k] = landed

    def b_step(origin, way):
        block = wall.at[x, origin, c, part_b]
        return send(block, block, at(dz=way), "b")

    def a_step(g, origin, way):
        group = wall.at[pl.ds(2 * g, 2), origin, c, part_a]
        return send(group, group, at(dz=way), "a")

    bm = [b_step(z, s)]
    bo = [b_step(z, -s)]
    top, bottom = pl.ds(0, ROWS // 2), pl.ds(ROWS // 2, ROWS // 2)
    up_y, down_y = lax.rem(y + 1, NY), lax.rem(y + NY - 1, NY)
    far_y = lax.rem(y + 2, NY)

    def cot(b, part, way):
        return send(call.at[b, part], call.at[b, part], at(dy=way), "cot")

    p_top = cot(y, top, 1)
    m_bottom = cot(y, bottom, -1)
    p_bottom = cot(y, bottom, 1)
    m_top = cot(y, top, -1)
    xb, xr = {0: b_across(0)}, {}
    scan = scan_chip(0, scan)

    def cot_share(b):
        return send(call.at[b], csib.at[b], at(dc=1), "cot2")

    cot_c = {0: cot_share(y)}
    am, ao = ([], []), ([], [])

    def serve_b(i):
        bm[i].wait_recv()
        if i < 3:
            bm.append(b_step(place(i + 1), s))
            bo[i].wait_recv()
            if i < 2:
                bo.append(b_step(place(-i - 1), -s))
            xb[-i - 1] = b_across(-i - 1)
        xb[i + 1] = b_across(i + 1)

    def serve_a0():
        await_all(wall.at[pl.ds(0, NX - 1), 0, 0, part_a], xa)
        for g in (0, 1):
            am[g].append(a_step(g, z, s))
            ao[g].append(a_step(g, z, -s))

    def serve_a(i):
        for g in (0, 1):
            am[g][i].wait_recv()
            if i < 3:
                am[g].append(a_step(g, place(i + 1), s))
                ao[g][i].wait_recv()
                if i < 2:
                    ao[g].append(a_step(g, place(-i - 1), -s))

    wsib = arrival()

    def share_b(k):
        await_all(wall.at[0, 0, 0, part_b], xr[k])
        group = wall.at[:, place(k), c, part_b]
        send(group, group, at(dc=1), "wshare", wsib)

    def share_a():
        group = wall.at[:, :, c, part_a]
        send(group, group, at(dc=1), "wshare", wsib)

    def intra(h):
        qh = phi(q_ref, h).astype(bf16)
        qf[:, cols(h)] = qh
        sc = jnp.where(causal(), nt(qh, kf[:, cols(h)]), 0.0).astype(bf16)
        scores[h] = sc
        att[:, cols(h)] = nn(sc, v_ref[:, cols(h)])

    for h in range(HEADS):
        intra(h)
    serve_b(0)
    serve_a0()
    b_relay(0)
    scan = scan_total(0, scan, False)
    serve_b(1)
    serve_a(0)
    b_relay(1)
    b_relay(-1)
    p_top.wait_recv()
    f_top = cot(down_y, top, 1)
    m_bottom.wait_recv()
    f_bottom = cot(up_y, bottom, -1)
    scan = scan_back(0, scan, False)
    serve_b(2)
    serve_a(1)
    b_relay(2)
    b_relay(-2)
    share_b(0)
    serve_b(3)
    serve_a(2)
    m_top.wait_recv()
    cot_c[1] = cot_share(up_y)
    b_relay(3)
    b_relay(-3)
    share_b(1)
    share_b(-1)
    scan = scan_share(0, scan)
    p_bottom.wait_recv()
    cot_c[3] = cot_share(down_y)
    b_relay(4)
    scan_end(0, scan, False)

    for h in range(HEADS):
        st = state[rows(h), :].astype(bf16)
        a = att[:, cols(h)] + nn(qf[:, cols(h)], st)
        r = lax.rsqrt(jnp.mean(a * a, axis=-1, keepdims=True) + EPS)
        u = a * r
        unit[:, cols(h)] = u
        inv[:, cols(h)] = jnp.broadcast_to(r, (ROWS, HD))
        n = u.astype(bf16)
        normed[:, cols(h)] = n
        prior[rows(h), :] = st
        t = u.T.astype(bf16)
        ntsend[h // 2, pl.ds((h % 2) * HD, HD), :] = t
    nt_copy = send(ntsend.at[1 - c], ntsib, at(dc=1), "nt")
    ntown[...] = ntsend[c]
    share_b(2)
    share_b(-2)
    serve_a(3)
    share_a()

    part_rows = HD // PARTS

    def products(j):
        b = lax.rem(y + j, NY)
        cot_c[j].wait_recv()
        p = nn(ntown[...], call[b]) + nn(ntsib[...], csib[b])
        for o in range(NZ):
            lanes = slice(o * HD, (o + 1) * HD)
            pz[j, o] = p[:HD, lanes]
            for g in range(PARTS):
                low = HD + g * part_rows
                xsend[g, j, o] = p[low : low + part_rows, lanes].astype(bf16)

    rm, ro = ([], []), ([], [])
    groups = ((0, 1, 3), (2,))

    def ring_send(g, i, way):
        count = pl.ds(0, len(groups[g]))
        return send(rsend.at[g, i, count], rrecv.at[g, i, count], at(dz=way), "ring")

    def ring(g, i):
        if i:
            rm[g][i - 1].wait_recv()
        far = zat(s * (4 - i))
        for n, j in enumerate(groups[g]):
            p = pz[j, far]
            if i:
                p = p + rrecv[g, i - 1, n].astype(f32)
            rsend[g, i, n] = p.astype(bf16)
        rm[g].append(ring_send(g, i, s))
        if i < 3:
            if i:
                ro[g][i - 1].wait_recv()
            far = zat(-s * (3 - i))
            for n, j in enumerate(groups[g]):
                p = pz[j, far]
                if i:
                    p = p + rrecv[g, 4 + i - 1, n].astype(f32)
                rsend[g, 4 + i, n] = p.astype(bf16)
            ro[g].append(ring_send(g, 4 + i, -s))

    def ring_end(g):
        rm[g][3].wait_recv()
        ro[g][2].wait_recv()
        for n, j in enumerate(groups[g]):
            t = pz[j, z] + rrecv[g, 3, n].astype(f32) + rrecv[g, 6, n].astype(f32)
            zown[j] = t
            esend[j] = t.astype(bf16)

    def place_of(dx):
        return lax.rem(x + dx - y + 2 * NX, NX)

    def x_send(g):
        landed = arrival()
        for j in (2, 1, 3):
            send(xsend.at[g, place_of(j)], xrecv.at[g, j - 1], at(dx=j), "x", landed)
        return landed

    def x_sum(g, landed):
        await_all(xrecv.at[g], landed)
        for o in range(NZ):
            t = xsend[g, place_of(0), o].astype(f32)
            for j in range(NX - 1):
                t = t + xrecv[g, j, o].astype(f32)
            xsum[g, o] = t
            dsend[g, o] = t.astype(bf16)
        landed = arrival()
        for j in range(1, NZ):
            send(dsend.at[g, zat(j)], drecv.at[g, j - 1], at(dz=j), "d", landed)
        return landed

    share_b(3)
    share_b(-3)
    share_b(4)
    nt_copy.wait_recv()
    products(0)
    products(1)
    products(3)
    ring(0, 0)
    f_top.wait_recv()
    f_bottom.wait_recv()
    cot_c[2] = cot_share(far_y)
    products(2)
    xs = [x_send(0)]
    ring(1, 0)
    xs += [x_send(g) for g in range(1, PARTS)]

    def weight(b):
        return wall[b].reshape(FEATS, WIDTH)

    await_all(wall.at[pl.ds(0, 2)], wsib)
    lsend[2] = nt(normed[...], weight(far_y)).astype(bf16)
    l_far = [
        send(lsend.at[2, top], lfar.at[0], at(dy=1), "layer"),
        send(lsend.at[2, bottom], lfar.at[1], at(dy=-1), "layer"),
    ]
    up = nn(call[0], weight(0))
    for b in range(1, NY):
        up = up + nn(call[b], weight(b))
    for h in range(HEADS):
        u = unit[:, cols(h)]
        d = up[:, h * HD : (h + 1) * HD]
        m = jnp.mean(d * u, axis=-1, keepdims=True)
        da = (inv[:, cols(h)] * (d - u * m)).astype(bf16)
        datt[:, cols(h)] = da
        state[rows(h), :] = tn(qf[:, cols(h)], da)
    scan = scan_begin(1)
    near = arrival()
    lout[0] = nt(normed[...], weight(up_y))
    lsend[0, bottom] = lout[0, bottom].astype(bf16)
    send(lsend.at[0, bottom], lrecv.at[0, bottom], at(dy=1), "layer", near)
    lout[1] = nt(normed[...], weight(down_y))
    lsend[1, top] = lout[1, top].astype(bf16)
    send(lsend.at[1, top], lrecv.at[1, top], at(dy=-1), "layer", near)

    def layer_pass():
        l_far[0].wait_recv()
        lsend[0, top] = (lout[0, top] + lfar[0].astype(f32)).astype(bf16)
        send(lsend.at[0, top], lrecv.at[0, top], at(dy=1), "layer", near)
        l_far[1].wait_recv()
        lsend[1, bottom] = (lout[1, bottom] + lfar[1].astype(f32)).astype(bf16)
        send(lsend.at[1, bottom], lrecv.at[1, bottom], at(dy=-1), "layer", near)
        lout[2] = nt(normed[...], weight(y))

    ring(0, 1)
    scan = scan_chip(1, scan)

    def grads(h):
        da = datt[:, cols(h)]
        vh = v_ref[:, cols(h)]
        ds = jnp.where(causal(), nt(da, vh), 0.0).astype(bf16)
        qg = nn(ds, kf[:, cols(h)]) + nt(da, prior[rows(h), :])
        qg_ref[:, cols(h)] = (qg * slope(q_ref, h)).astype(bf16)
        kacc[:, cols(h)] = tn(ds, qf[:, cols(h)])
        vacc[:, cols(h)] = tn(scores[h], da)

    ring(1, 1)
    ring(0, 2)
    for h in range(HEADS):
        grads(h)
    outs = [load(0, qg_ref, qg_hbm)]
    ds = [x_sum(0, xs[0])]
    ring(1, 2)
    scan = scan_total(1, scan, True)
    ring(0, 3)
    ds.append(x_sum(1, xs[1]))
    layer_pass()
    ring(1, 3)
    ds.append(x_sum(2, xs[2]))
    scan = scan_back(1, scan, True)
    ring_end(0)
    ring_end(1)
    landed_e = arrival()
    for j in range(1, NX):
        send(esend.at[place_of(j)], erecv.at[j - 1], at(dx=j), "e", landed_e)
    ds.append(x_sum(3, xs[3]))
    scan = scan_share(1, scan)
    await_all(erecv, landed_e)
    t = zown[place_of(0)]
    for j in range(NX - 1):
        t = t + erecv[j].astype(f32)
    mine[:, pl.ds(0, HD)] = t.T
    for g, landed in enumerate(ds):
        await_all(drecv.at[g], landed)
        t = xsum[g, z]
        for j in range(NZ - 1):
            t = t + drecv[g, j].astype(f32)
        xsum[g, z] = t
    mine[:, pl.ds(HD, HD)] = jnp.concatenate([xsum[g, z] for g in range(PARTS)], axis=0).T
    other = pl.multiple_of((1 - c) * WROWS, WROWS)
    last = send(mine.at[pl.ds(other, WROWS)], tsib_recv, at(dc=1), "last")
    scan_end(1, scan, True)
    for h in range(HEADS):
        st = state[rows(h), :].astype(bf16)
        kg = kacc[:, cols(h)] + nt(v_ref[:, cols(h)], st)
        kg_ref[:, cols(h)] = (kg * slope(k_ref, h)).astype(bf16)
        vg_ref[:, cols(h)] = (vacc[:, cols(h)] + nn(kf[:, cols(h)], st)).astype(bf16)

    outs += [load(1, kg_ref, kg_hbm), load(2, vg_ref, vg_hbm)]
    await_all(lrecv, near)
    lo_ref[...] = (lout[2] + lrecv[0].astype(f32) + lrecv[1].astype(f32)).astype(bf16)

    outs.append(load(3, lo_ref, lo_hbm))
    last.wait_recv()
    here = mine[pl.ds(pl.multiple_of(c * WROWS, WROWS), WROWS), :] * grad_scale
    there = tsib_recv[...] * grad_scale
    dw_ref[:, pl.ds(0, 2 * HD)] = jnp.where(c == 0, here, there)
    dw_ref[:, pl.ds(2 * HD, 2 * HD)] = jnp.where(c == 0, there, here)
    outs.append(load(4, dw_ref, dw_hbm))
    sent("own", own_b)
    sent("chip", zrecv.at[:, pl.ds(0, NZ - 1)])
    sent("total", trecv.at[:, pl.ds(0, NX - 1)])
    sent("back", psend.at[:, pl.ds(0, NZ - 1)])
    sent("share", pre.at[:, pl.ds(0, half)])
    sent("xa", wall.at[pl.ds(0, NX - 1), 0, 0, part_a])
    sent("b", wall.at[0, pl.ds(0, NZ - 1), 0, part_b])
    sent("bx", wall.at[pl.ds(0, 2), :, 0, part_b])
    sent("br", wall.at[0, :, 0, part_b])
    sent("a", wall.at[:, pl.ds(0, NZ - 1), 0, part_a])
    sent("wshare", wall.at[pl.ds(0, 2)])
    sent("cot", call.at[pl.ds(0, 3)])
    sent("cot2", call)
    sent("nt", ntsib)
    sent("layer", lsend)
    sent("ring", rsend.at[:, :, pl.ds(0, 2)])
    sent("x", xrecv)
    sent("d", drecv)
    sent("e", erecv)
    sent("last", tsib_recv)
    for copy in outs:
        copy.wait()
    assert not kinds and len(arrivals) == ARRIVALS


def write_out(*refs):
    ins, outs, bufs, (here, there) = refs[:5], refs[5:10], refs[10:15], refs[15:]

    def start(i, src, dst, sem):
        copy = pltpu.make_async_copy(src, dst, sem.at[i])
        copy.start()
        return copy

    coming = [start(i, ins[i], bufs[i], here) for i in range(5)]
    going = []
    for i in (4, 1, 2, 3, 0):
        coming[i].wait()
        going.append(start(i, bufs[i], outs[i], there))
    for copy in going:
        copy.wait()


def solution(mesh):
    split = Mesh(mesh.devices.reshape(NX, NZ, NC, NY), (*SEQ, "head"))
    placed = P(SEQ, "head")

    def shards(q, k, v, w, cot):
        shape = jax.ShapeDtypeStruct
        vm = pltpu.VMEM
        found = pl.pallas_call(
            functools.partial(kernel, 16384.0**-0.5),
            out_shape=(
                shape((ROWS, FEATS), bf16),
                shape((ROWS, WIDTH), bf16),
                shape((ROWS, WIDTH), bf16),
                shape((ROWS, WIDTH), bf16),
                shape((WROWS, WIDTH), f32),
            ),
            in_specs=[pl.BlockSpec(memory_space=pltpu.HBM)] * 5,
            out_specs=[pl.BlockSpec(memory_space=pltpu.HBM)] * 5,
            scratch_shapes=[
                vm((ROWS, FEATS), bf16),
                vm((ROWS, WIDTH), bf16),
                vm((ROWS, WIDTH), bf16),
                vm((ROWS, WIDTH), bf16),
                vm((WROWS, WIDTH), f32),
                vm((ROWS, WIDTH), bf16),
                vm((ROWS, WIDTH), bf16),
                vm((ROWS, WIDTH), bf16),
                vm((ROWS, WIDTH), bf16),
                vm((ROWS, WIDTH), bf16),
                vm((HEADS, ROWS, ROWS), bf16),
                vm((ROWS, WIDTH), f32),
                vm((ROWS, WIDTH), f32),
                vm((ROWS, WIDTH), f32),
                vm((ROWS, WIDTH), bf16),
                vm((ROWS, WIDTH), bf16),
                vm((WIDTH, HD), bf16),
                vm((ROWS, WIDTH), f32),
                vm((ROWS, WIDTH), f32),
                vm((WIDTH, HD), f32),
                vm((2, WIDTH, HD), bf16),
                vm((2, WIDTH, HD), bf16),
                vm((2, 2 * HD, HD), bf16),
                vm((2, NZ, 2 * HD // NZ, HD), bf16),
                vm((2, 2 * HD // NZ, HD), bf16),
                vm((2, NX, 2 * HD // NZ, HD), bf16),
                vm((2, NZ, 2 * HD // NZ, HD), bf16),
                vm((2, WIDTH, HD), bf16),
                vm((NX, NZ, NC, WROWS, WIDTH), bf16),
                vm((NY, ROWS, FEATS), bf16),
                vm((NY, ROWS, FEATS), bf16),
                vm((3, ROWS, FEATS), f32),
                vm((3, ROWS, FEATS), bf16),
                vm((2, ROWS, FEATS), bf16),
                vm((2, ROWS // 2, FEATS), bf16),
                vm((2 * HD, ROWS), bf16),
                vm((2, 2 * HD, ROWS), bf16),
                vm((2 * HD, ROWS), bf16),
                vm((NX, NZ, HD, HD), f32),
                vm((PARTS, NX, NZ, HD // PARTS, HD), bf16),
                vm((PARTS, NX - 1, NZ, HD // PARTS, HD), bf16),
                vm((PARTS, NZ, HD // PARTS, HD), f32),
                vm((PARTS, NZ, HD // PARTS, HD), bf16),
                vm((PARTS, NZ - 1, HD // PARTS, HD), bf16),
                vm((2, 7, 3, HD, HD), bf16),
                vm((2, 7, 3, HD, HD), bf16),
                vm((NX, HD, HD), f32),
                vm((NX, HD, HD), bf16),
                vm((NX - 1, HD, HD), bf16),
                vm((HD, 2 * HD), f32),
                vm((WROWS, 2 * HD), f32),
                pltpu.SemaphoreType.DMA((DEPARTURES,)),
                pltpu.SemaphoreType.DMA((ARRIVALS,)),
                pltpu.SemaphoreType.DMA((5,)),
            ],
            compiler_params=pltpu.CompilerParams(
                collective_id=0, has_side_effects=True, vmem_limit_bytes=56 * 2**20
            ),
            name="layer_step",
        )(q, k, v, w, cot)
        return pl.pallas_call(
            write_out,
            out_shape=[shape(a.shape, a.dtype) for a in found],
            in_specs=[pl.BlockSpec(memory_space=pltpu.HBM)] * 5,
            out_specs=[pl.BlockSpec(memory_space=pltpu.HBM)] * 5,
            scratch_shapes=[
                *(vm(a.shape, a.dtype) for a in found),
                pltpu.SemaphoreType.DMA((5,)),
                pltpu.SemaphoreType.DMA((5,)),
            ],
            name="write_out",
        )(*found)

    return jax.shard_map(
        shards, mesh=split, in_specs=(placed,) * 5, out_specs=(placed,) * 5, check_vma=False
    )
```
